256 devices in a mesh: rep: 8 (over z_lo, core), fsdp: 32 (over z_hi, x, y).
Axes of the slice: x: 4, y: 4, z: 8 (z_hi: 2, z_lo: 4; z = z_hi * 4 + z_lo), core: 2. Of those that a mesh axis runs over, the one named last changes fastest.
Arguments:
- inputs: bfloat16 [32768, 8192], P(('rep', 'fsdp')), may hold values from -6 to 6
- value_weight: bfloat16 [8192, 512], P('fsdp'), may hold values from -0.0625 to 0.0625
- send_slot: int32 [32768], P(('rep', 'fsdp')), may hold values from 0 to 255, as said below
- response_id: int32 [32768], P(('rep', 'fsdp')), may hold values from 0 to 127, as said below
- queries: bfloat16 [65536, 4096], P(('rep', 'fsdp')), may hold values from -6 to 6
- keys: bfloat16 [65536, 512], P(('rep', 'fsdp')), may hold values from -6 to 6
- upstream: bfloat16 [65536, 4096], P(('rep', 'fsdp')), may hold values from -6 to 6
Outputs:
- grad_inputs: bfloat16 [32768, 8192], P(('rep', 'fsdp'))
- grad_queries: bfloat16 [65536, 4096], P(('rep', 'fsdp'))
- grad_keys: bfloat16 [65536, 512], P(('rep', 'fsdp'))
- grad_weight: bfloat16 [8192, 512], P('fsdp')
The draws below stay inside these ranges and needn't reach their ends.
Inputs may be any that keep to these rules, and one draw needn't show every extreme that they name: `send_slot`: on each device the rows form aligned runs of 8; a run goes whole to one peer, to slots peer * 8 + 0 .. 7 in row order; no two runs of a device share a peer; the first run of every device stays on the device itself. `response_id`: rows of one response are consecutive, lie within one run, and number at most 8; the first run of every device is one response of 8 rows; the last row of every device is a response of its own.
All inputs are finite; a program needn't handle non-finite values.
Results may differ from the reference program's by a relative error of at most 0.012.
Values may be sent and summed in bfloat16 or wider, within the bound.
No kernel may reach another device: no remote copies, remote signals or barrier semaphores. Data moves between devices by JAX's collectives and lax.ppermute only.
A program may use at most 128 MiB of HBM per device.

```python
import jax
import jax.numpy as jnp
from jax import lax

D = 8192
KVH = 4
GROUP = 8
HD = 128
CAP = 8
QH = 32
WIDTH = 512
ROWS = 128
SLOTS = 256
TOKENS = 32768
ALLSLOTS = 65536
N_FSDP = 32


def plan_tables(key):
    devices = TOKENS // ROWS
    peers = SLOTS // CAP
    blocks = ROWS // CAP
    key_order, key_cuts = jax.random.split(key)
    own = jnp.arange(devices, dtype=jnp.int32) % peers
    lanes = jnp.arange(peers, dtype=jnp.int32)
    scores = jax.random.randint(key_order, (devices, peers), 0, 2 ** 20) * peers + lanes[None, :]
    scores = jnp.where(lanes[None, :] == own[:, None], -1, scores)
    order = jnp.argsort(scores, axis=1, stable=True).astype(jnp.int32)
    dest = order[:, :blocks]
    places = jnp.arange(CAP, dtype=jnp.int32)
    slots = (dest[:, :, None] * CAP + places[None, None, :]).reshape(TOKENS).astype(jnp.int32)
    coins = jax.random.randint(key_cuts, (devices, blocks, CAP), 0, 3) == 0
    later = (jnp.arange(blocks) > 0)[None, :, None]
    position = jnp.arange(ROWS, dtype=jnp.int32).reshape(1, blocks, CAP)
    cuts = (places == 0)[None, None, :] | coins & later | (position == ROWS - 1)
    starts = jnp.where(cuts, position, 0).reshape(devices, ROWS)
    ids = lax.cummax(starts, axis=1).reshape(TOKENS).astype(jnp.int32)
    return (slots, ids)


def draw_send_slot(key, part):
    slots, ids = plan_tables(key)
    return slots


def draw_response_id(key, part):
    slots, ids = plan_tables(key)
    return ids


def shard_levels(stream_key, shape, cuts, least, largest):
    level = 1.0
    for axis_at, blocks in cuts:
        draws = jax.random.uniform(jax.random.fold_in(jax.random.fold_in(stream_key, 6), axis_at), (blocks,), jnp.float32, least / len(cuts), largest / len(cuts))
        level = level * jnp.repeat(jnp.exp(draws), shape[axis_at] // blocks).reshape((-1,) + (1,) * (len(shape) - 1 - axis_at))
    return level


def noise(key, extent, scale, limit, cuts=(), kind=jnp.bfloat16):
    array = jax.random.normal(key, extent, jnp.float32) * scale
    if len(cuts) > 0:
        array = shard_levels(key, extent, cuts, -0.22, 0.18) * array
    return jnp.clip(array, min=-limit, max=limit).astype(kind)


def setup_inputs(seed: int = 0) -> dict:
    splits = jax.random.split(jax.random.key(seed), 8)
    return {
        "inputs": noise(splits[0], (TOKENS, D), 1.0, 6.0, ((0, 256),)),
        "value_weight": noise(splits[1], (D, WIDTH), D ** -0.5, 0.0625, ((0, 32),)),
        "send_slot": draw_send_slot(jax.random.fold_in(splits[7], 71), 0),
        "response_id": draw_response_id(jax.random.fold_in(splits[7], 71), 0),
        "queries": noise(splits[4], (ALLSLOTS, QH * HD), 1.0, 6.0, ((0, 256),)),
        "keys": noise(splits[5], (ALLSLOTS, WIDTH), 1.0, 6.0, ((0, 256),)),
        "upstream": noise(splits[6], (ALLSLOTS, QH * HD), 1.0, 6.0, ((0, 256),)),
    }


def reference(inputs, value_weight, send_slot, response_id, queries, keys, upstream):
    scale = 1.0 / (HD ** 0.5)
    row = jnp.arange(TOKENS, dtype=jnp.int32)
    device = row // ROWS
    group = device // N_FSDP
    source = device % N_FSDP
    target = ((group * N_FSDP + send_slot // CAP) * N_FSDP + source) * CAP + send_slot % CAP
    target = target.astype(jnp.int32)
    row_values = jnp.dot(inputs, value_weight, preferred_element_type=jnp.float32).astype(jnp.bfloat16)
    values = jnp.zeros((ALLSLOTS, WIDTH), jnp.bfloat16).at[target].set(row_values)
    slot_id = jnp.full((ALLSLOTS,), -1, jnp.int32).at[target].set(response_id)
    blocks = ALLSLOTS // CAP
    qry = queries.reshape(blocks, CAP, KVH, GROUP, HD).astype(jnp.float32)
    key_f = keys.reshape(blocks, CAP, KVH, HD).astype(jnp.float32)
    val_f = values.reshape(blocks, CAP, KVH, HD).astype(jnp.float32)
    grad_out = upstream.reshape(blocks, CAP, KVH, GROUP, HD).astype(jnp.float32)
    ids = slot_id.reshape(blocks, CAP)
    lower = jnp.arange(CAP)[None, :] <= jnp.arange(CAP)[:, None]
    visible = (ids[:, :, None] == ids[:, None, :]) & lower[None]
    visible = visible[:, None, None]
    scores = jnp.einsum('bikgd,bjkd->bkgij', qry, key_f) * scale
    masked = jnp.where(visible, scores, -1e30)
    top = jnp.max(masked, axis=-1, keepdims=True)
    expo = jnp.where(visible, jnp.exp(masked - top), 0.0)
    probs = expo / jnp.sum(expo, axis=-1, keepdims=True)
    probs_low = probs.astype(jnp.bfloat16).astype(jnp.float32)
    dprob = jnp.einsum('bikgd,bjkd->bkgij', grad_out, val_f)
    delta = jnp.sum(probs * dprob, axis=-1, keepdims=True)
    dscore = (probs * (dprob - delta)).astype(jnp.bfloat16).astype(jnp.float32)
    grad_q = (jnp.einsum('bkgij,bjkd->bikgd', dscore, key_f) * scale).astype(jnp.bfloat16)
    grad_k = (jnp.einsum('bkgij,bikgd->bjkd', dscore, qry) * scale).astype(jnp.bfloat16)
    grad_v = jnp.einsum('bkgij,bikgd->bjkd', probs_low, grad_out).astype(jnp.bfloat16)
    row_grad = grad_v.reshape(ALLSLOTS, WIDTH)[target]
    grad_inputs = jnp.dot(row_grad, value_weight.T, preferred_element_type=jnp.float32).astype(jnp.bfloat16)
    grad_weight = jnp.dot(inputs.T, row_grad, preferred_element_type=jnp.float32).astype(jnp.bfloat16)
    return (grad_inputs, grad_q.reshape(ALLSLOTS, QH * HD), grad_k.reshape(ALLSLOTS, WIDTH), grad_weight)
```

```python
import functools

import jax
import jax.numpy as jnp
from jax import lax
from jax.experimental import pallas as pl
from jax.experimental.pallas import tpu as pltpu
from jax.sharding import PartitionSpec as P

KVH = 4
GROUP = 8
HD = 128
AXES = ("rep", "fsdp")
F32 = jnp.float32
BF16 = jnp.bfloat16
NZL, NCO, NZH, NX, NY = 4, 2, 2, 4, 4


def permute(array, move):
    pairs = []
    for e in range(NZL * NCO * NZH * NX * NY):
        place = (e // 64, e // 32 % 2, e // 16 % 2, e // 4 % 4, e % 4)
        zl, co, zh, x, y = move(*place)
        pairs.append((e, (((zl * NCO + co) * NZH + zh) * NX + x % NX) * NY + y % NY))
    return lax.ppermute(array, AXES, pairs)


def along_y(k):
    return lambda zl, co, zh, x, y: (zl, co, zh, x, y + k)


def along_x(k):
    return lambda zl, co, zh, x, y: (zl, co, zh, x + k, y)


def other_core(zl, co, zh, x, y):
    return zl, 1 - co, zh, x, y


def mirror(zl, co, zh, x, y):
    return NZL - 1 - zl, co, 1 - zh, x, y


def flip_zl(bit):
    return lambda zl, co, zh, x, y: (zl ^ bit, co, zh, x, y)


def column_blocks(place, k):
    co, zh, x, y = place[0], place[1], place[2], place[3]
    for zr in range(NZH):
        for xr in range(NX):
            for cr in range(NCO):
                z = zh + zr - 2 * zh * zr
                c = co + cr - 2 * co * cr
                block = ((z * NX + lax.rem(x - xr + NX, NX)) * NY + lax.rem(y + k, NY)) * NCO + c
                yield (zr * NX + xr) * NCO + cr, block


def split_kernel(place, full, *parts):
    for k, part in enumerate(parts):
        for at, block in column_blocks(place, k):
            part[:, at * 128 : (at + 1) * 128] = full[:, pl.ds(pl.multiple_of(block * 128, 128), 128)]


def join_kernel(place, *refs):
    full = refs[-1]
    for k, part in enumerate(refs[:-1]):
        for at, block in column_blocks(place, k):
            full[:, pl.ds(pl.multiple_of(block * 128, 128), 128)] = part[:, at * 128 : (at + 1) * 128]


def split_columns(place, full):
    rows, width = full.shape
    return pl.pallas_call(
        split_kernel,
        out_shape=[jax.ShapeDtypeStruct((rows, width // NY), full.dtype)] * NY,
        in_specs=[pl.BlockSpec(memory_space=pltpu.SMEM), pl.BlockSpec(memory_space=pltpu.VMEM)],
        out_specs=[pl.BlockSpec(memory_space=pltpu.VMEM)] * NY,
        compiler_params=pltpu.CompilerParams(vmem_limit_bytes=16 * 1024 * 1024),
        name="split_columns",
    )(place, full)


def join_columns(place, parts):
    rows, width = parts[0].shape
    return pl.pallas_call(
        join_kernel,
        out_shape=jax.ShapeDtypeStruct((rows, width * NY), parts[0].dtype),
        in_specs=[pl.BlockSpec(memory_space=pltpu.SMEM)] + [pl.BlockSpec(memory_space=pltpu.VMEM)] * NY,
        out_specs=pl.BlockSpec(memory_space=pltpu.VMEM),
        compiler_params=pltpu.CompilerParams(vmem_limit_bytes=16 * 1024 * 1024),
        name="join_columns",
    )(place, *parts)


def block_attention(queries, keys, values, upstream, slot_id, peers, cap):
    scale = 1.0 / HD**0.5
    qry = queries.reshape(peers, cap, KVH, GROUP, HD)
    key_b = keys.reshape(peers, cap, KVH, HD)
    val_b = values.reshape(peers, cap, KVH, HD)
    grad_out = upstream.reshape(peers, cap, KVH, GROUP, HD)
    ids = slot_id.reshape(peers, cap)
    lower = jnp.arange(cap)[None, :] <= jnp.arange(cap)[:, None]
    visible = ((ids[:, :, None] == ids[:, None, :]) & lower[None])[:, None, None]
    scores = jnp.einsum("bikgd,bjkd->bkgij", qry, key_b, preferred_element_type=F32) * scale
    masked = jnp.where(visible, scores, -1e30)
    top = jnp.max(masked, axis=-1, keepdims=True)
    expo = jnp.where(visible, jnp.exp(masked - top), 0.0)
    probs = expo / jnp.sum(expo, axis=-1, keepdims=True)
    probs_low = probs.astype(BF16)
    dprob = jnp.einsum("bikgd,bjkd->bkgij", grad_out, val_b, preferred_element_type=F32)
    delta = jnp.sum(probs * dprob, axis=-1, keepdims=True)
    dscore = (probs * (dprob - delta)).astype(BF16)
    grad_q = (jnp.einsum("bkgij,bjkd->bikgd", dscore, key_b, preferred_element_type=F32) * scale).astype(BF16)
    grad_k = (jnp.einsum("bkgij,bikgd->bjkd", dscore, qry, preferred_element_type=F32) * scale).astype(BF16)
    grad_v = jnp.einsum("bkgij,bikgd->bjkd", probs_low, grad_out, preferred_element_type=F32).astype(BF16)
    total_rows = peers * cap
    return (
        grad_q.reshape(total_rows, KVH * GROUP * HD),
        grad_k.reshape(total_rows, KVH * HD),
        grad_v.reshape(total_rows, KVH * HD),
    )


def dot(a, b, dims):
    return lax.dot_general(a, b, (dims, ((), ())), preferred_element_type=F32)


def body(inputs, value_weight, send_slot, response_id, queries, keys, upstream):
    peers = lax.axis_size("fsdp")
    slots = queries.shape[0]
    cap = slots // peers
    half, width = value_weight.shape[0] // NCO, value_weight.shape[1]
    rep, fsdp = lax.axis_index("rep"), lax.axis_index("fsdp")
    core = rep % NCO
    place = jnp.stack([core, fsdp // (NX * NY), fsdp // NY % NX, fsdp % NY]).astype(jnp.int32)

    id_buffer = jnp.full((slots,), -1, jnp.int32).at[send_slot].set(response_id)
    slot_id = lax.all_to_all(id_buffer, "fsdp", split_axis=0, concat_axis=0, tiled=True)

    pieces = split_columns(place, inputs)
    pieces = [pieces[0]] + [permute(pieces[k], along_y(k)) for k in range(1, NY)]
    own = lax.dynamic_slice_in_dim(value_weight, core * half, half, 0)
    pair = jnp.stack([own, permute(own, mirror)])
    line = jnp.stack([pair] + [permute(pair, along_x(k)) for k in range(1, NX)], axis=1)
    weight = jnp.stack([line, permute(line, other_core)], axis=2).reshape(-1, width)

    partial = [dot(piece, weight, ((1,), (0,))) for piece in pieces]
    projected = partial[0]
    for k in range(1, NY):
        projected += permute(partial[k].astype(BF16), along_y(-k)).astype(F32)
    value_buffer = jnp.zeros((slots, width), BF16).at[send_slot].set(projected.astype(BF16))
    values = lax.all_to_all(value_buffer, "fsdp", split_axis=0, concat_axis=0, tiled=True)

    grad_q, grad_k, grad_v = block_attention(queries, keys, values, upstream, slot_id, peers, cap)

    returned = lax.all_to_all(grad_v, "fsdp", split_axis=0, concat_axis=0, tiled=True)
    row_grad = returned[send_slot]
    grads = [row_grad] + [permute(row_grad, along_y(k)) for k in range(1, NY)]

    back = [dot(grad, weight, ((1,), (1,))).astype(BF16) for grad in grads]
    back = [back[0]] + [permute(back[k], along_y(-k)) for k in range(1, NY)]
    grad_inputs = join_columns(place, back)

    share = sum(dot(piece, grad, ((0,), (0,))) for piece, grad in zip(pieces, grads, strict=True))
    share = share.reshape(NZH, NX, NCO, half, width)
    share = share[:, :, 0] + permute(share[:, :, 1].astype(BF16), other_core).astype(F32)
    total = share[:, 0]
    for k in range(1, NX):
        total += permute(share[:, k].astype(BF16), along_x(-k)).astype(F32)
    total = total[0] + permute(total[1].astype(BF16), mirror).astype(F32)
    total += permute(total, flip_zl(1))
    total += permute(total, flip_zl(2))
    mine = total.astype(BF16)
    other = permute(mine, other_core)
    first = jnp.where(core == 0, mine, other)
    second = jnp.where(core == 0, other, mine)
    grad_weight = jnp.concatenate([first, second], axis=0)
    return grad_inputs, grad_q, grad_k, grad_weight


def solution(mesh):
    spread, sharded = P(("rep", "fsdp"), None), P("fsdp", None)
    line = P(("rep", "fsdp"))
    return jax.shard_map(
        body,
        mesh=mesh,
        in_specs=(spread, sharded, line, line, spread, spread, spread),
        out_specs=(spread, spread, spread, sharded),
        check_vma=False,
    )
```

```python
import jax
import jax.numpy as jnp
from jax import lax
from jax.experimental import pallas as pl
from jax.experimental.pallas import tpu as pltpu
from jax.sharding import PartitionSpec as P

KVH = 4
GROUP = 8
HD = 128
CAP = 8
TILE = 128
BLOCKS = TILE // CAP
AXES = ("rep", "fsdp")
F32 = jnp.float32
BF16 = jnp.bfloat16
NZL, NCO, NZH, NX, NY = 4, 2, 2, 4, 4
SLICES = NZH * NX
TOKEN = jax.ShapeDtypeStruct((8, 128), jnp.float32)
VMEM = pl.BlockSpec(memory_space=pltpu.VMEM)
ANY = pl.BlockSpec(memory_space=pl.ANY)


def permute(array, move):
    pairs = []
    for e in range(NZL * NCO * NZH * NX * NY):
        place = (e // 64, e // 32 % 2, e // 16 % 2, e // 4 % 4, e % 4)
        zl, co, zh, x, y = move(*place)
        pairs.append((e, (((zl * NCO + co) * NZH + zh) * NX + x % NX) * NY + y % NY))
    return lax.ppermute(array, AXES, pairs)


def along_y(k):
    return lambda zl, co, zh, x, y: (zl, co, zh, x, y + k)


def along_x(k):
    return lambda zl, co, zh, x, y: (zl, co, zh, x + k, y)


def other_core(zl, co, zh, x, y):
    return zl, 1 - co, zh, x, y


def mirror(zl, co, zh, x, y):
    return NZL - 1 - zl, co, 1 - zh, x, y


def flip_zl(bit):
    return lambda zl, co, zh, x, y: (zl ^ bit, co, zh, x, y)


def call(kernel, name, out, *args, ins=None, outs=None, scratch=(), mib=4, flops=0):
    size = sum(a.size * a.dtype.itemsize for a in args) + sum(o.size * o.dtype.itemsize for o in out)
    return pl.pallas_call(
        kernel,
        out_shape=out,
        in_specs=[VMEM] * len(args) if ins is None else ins,
        out_specs=[VMEM] * len(out) if outs is None else outs,
        scratch_shapes=scratch,
        compiler_params=pltpu.CompilerParams(vmem_limit_bytes=mib * 1024 * 1024),
        cost_estimate=pl.CostEstimate(flops=flops, bytes_accessed=size, transcendentals=0),
        name=name,
    )(*args)


def fetch(sources, targets, sems):
    copies = [pltpu.make_async_copy(s, t, sems.at[i]) for i, (s, t) in enumerate(zip(sources, targets, strict=True))]
    for copy in copies:
        copy.start()
    return copies


def at_place():
    rep, fsdp = lax.axis_index("rep"), lax.axis_index("fsdp")
    return lax.rem(rep, NCO), lax.div(fsdp, NX * NY), lax.rem(lax.div(fsdp, NY), NX), lax.rem(fsdp, NY)


def like(shape, dtype):
    return jax.ShapeDtypeStruct(shape, dtype)


def dot(a, b, over):
    return lax.dot_general(a, b, (((over[0],), (over[1],)), ((), ())), preferred_element_type=F32)


def feature_blocks(k):
    core, zh, x, y = at_place()
    for zr in range(NZH):
        for xr in range(NX):
            z = zh + zr - 2 * zh * zr
            slice_at = (z * NX + lax.rem(x - xr + NX, NX)) * NY + lax.rem(y + k, NY)
            for cr in range(NCO):
                yield (zr * NX + xr) * NCO + cr, slice_at * NCO + core + cr - 2 * core * cr


def finish(token):
    token[...] = jnp.zeros(token.shape, token.dtype)


def masks_kernel(slots_in, ids_in, after, masks, slots, ids, sems):
    copies = fetch((slots_in, ids_in), (slots, ids), sems)
    lane = lax.broadcasted_iota(jnp.int32, (CAP, TILE), 1) & (CAP - 1)
    sub = lax.broadcasted_iota(jnp.int32, (CAP, TILE), 0)
    causal = sub <= lane
    plain = causal.astype(jnp.int32)
    for p in range(masks.shape[0]):
        masks[p] = plain
    for copy in copies:
        copy.wait()
    for r in range(slots.shape[0] // CAP):
        keys = jnp.zeros((CAP, TILE), jnp.int32)
        rows = jnp.zeros((CAP, TILE), jnp.int32)
        for j in range(CAP):
            value = ids[r * CAP + j]
            keys = jnp.where(sub == j, value, keys)
            rows = jnp.where(lane == j, value, rows)
        masks[lax.div(slots[r * CAP], CAP)] = jnp.where((keys == rows) & causal, 1, 0)


def run_masks(slots, ids, peers, after):
    index = pltpu.SMEM(slots.shape, jnp.int32)
    scratch = (index, index, pltpu.SemaphoreType.DMA((2,)))
    out = [like((peers, CAP, TILE), jnp.int32)]
    return call(masks_kernel, "masks", out, slots, ids, after, ins=[ANY] * 3, scratch=scratch, mib=56)[0]


def split_kernel(full_in, weight_in, p0, p1, p2, p3, weight, full, sems):
    rows = weight.shape[0]
    here = weight_in.at[pl.ds(pl.multiple_of(at_place()[0] * rows, rows), rows)]
    copies = fetch((full_in, here), (full, weight), sems)
    copies[0].wait()
    width = full.shape[1] // (NY * SLICES * NCO)
    for k, part in enumerate((p0, p1, p2, p3)):
        for at, block in feature_blocks(k):
            part[:, at * width : (at + 1) * width] = full[:, pl.ds(pl.multiple_of(block * width, width), width)]
    copies[1].wait()


def split(full, weight):
    rows, columns = full.shape
    out = [like((rows, columns // NY), full.dtype)] * NY + [like((weight.shape[0] // NCO, weight.shape[1]), weight.dtype)]
    scratch = (pltpu.VMEM(full.shape, full.dtype), pltpu.SemaphoreType.DMA((2,)))
    return call(split_kernel, "split", out, full, weight, ins=[ANY] * 2, scratch=scratch, mib=56)


def join_kernel(p0, p1, p2, p3, full, token):
    finish(token)
    width = p0.shape[1] // (SLICES * NCO)
    for k, part in enumerate((p0, p1, p2, p3)):
        for at, block in feature_blocks(k):
            full[:, pl.ds(pl.multiple_of(block * width, width), width)] = part[:, at * width : (at + 1) * width]


def join(parts):
    rows, columns = parts[0].shape
    return call(join_kernel, "join", [like((rows, columns * NY), parts[0].dtype), TOKEN], *parts, mib=56)


def heads(block, t):
    rows = block[t * TILE : (t + 1) * TILE, :]
    return jnp.concatenate([rows[:, h * HD : (h + 1) * HD] for h in range(GROUP)], axis=0)


def own_block(lanes):
    return lax.broadcasted_iota(jnp.int32, (CAP, lanes), 1) % TILE // CAP


def fold(pairs, block):
    out = pairs[0:CAP]
    for b in range(1, BLOCKS):
        out = jnp.where(block == b, pairs[b * CAP : (b + 1) * CAP], out)
    return out


def unfold(folded, block):
    return jnp.concatenate([jnp.where(block == b, folded, 0.0) for b in range(BLOCKS)], axis=0).astype(BF16)


def scores_kernel(queries, keys, scores):
    block = own_block(GROUP * TILE)
    for t in range(scores.shape[1]):
        pairs = dot(keys[t * TILE : (t + 1) * TILE, :], heads(queries, t), (1, 1))
        scores[0, t] = fold(pairs, block)


def probs_kernel(scores, masks, upstream, *rest):
    grad_v, probs = rest[-2:]
    small, block = own_block(TILE), own_block(GROUP * TILE)
    for t in range(scores.shape[1]):
        mask = masks[t * BLOCKS]
        for b in range(1, BLOCKS):
            mask = jnp.where(small == b, masks[t * BLOCKS + b], mask)
        visible = jnp.concatenate([mask] * GROUP, axis=1) != 0
        masked = jnp.where(visible, scores[0, t] * (1.0 / HD**0.5), -1e30)
        top = jnp.max(masked, axis=0, keepdims=True)
        expo = jnp.where(visible, jnp.exp(masked - top), 0.0)
        prob = expo / jnp.sum(expo, axis=0, keepdims=True)
        probs[0, t] = prob
        grad = dot(unfold(prob, block), heads(upstream, t), (1, 0))
        grad_v[t * TILE : (t + 1) * TILE, :] = grad.astype(BF16)


def dscore_kernel(probs, values, upstream, queries, keys, grad_q, grad_k, token):
    finish(token)
    scale = 1.0 / HD**0.5
    block = own_block(GROUP * TILE)
    for t in range(probs.shape[1]):
        rows = slice(t * TILE, (t + 1) * TILE)
        prob = probs[0, t]
        dprob = fold(dot(values[rows, :], heads(upstream, t), (1, 1)), block)
        delta = jnp.sum(prob * dprob, axis=0, keepdims=True)
        dscore = unfold(prob * (dprob - delta), block)
        grad_k[rows, :] = (dot(dscore, heads(queries, t), (1, 0)) * scale).astype(BF16)
        grad = (dot(dscore, keys[rows, :], (0, 0)) * scale).astype(BF16)
        for h in range(GROUP):
            grad_q[rows, h * HD : (h + 1) * HD] = grad[h * TILE : (h + 1) * TILE]


def per_head(kernel, name, ins, outs, args, flops):
    size = sum(a.size * a.dtype.itemsize for a in args) + sum(o.size * o.dtype.itemsize for o, _ in outs)
    return pl.pallas_call(
        kernel,
        grid=(KVH,),
        out_shape=[o for o, _ in outs],
        in_specs=ins,
        out_specs=[s for _, s in outs],
        compiler_params=pltpu.CompilerParams(vmem_limit_bytes=56 * 1024 * 1024),
        cost_estimate=pl.CostEstimate(flops=flops, bytes_accessed=size, transcendentals=0),
        name=name,
    )(*args)


def attention_specs(slots):
    wide = pl.BlockSpec((slots, GROUP * HD), lambda k: (0, k))
    narrow = pl.BlockSpec((slots, HD), lambda k: (0, k))
    tiles = slots // TILE
    folded = pl.BlockSpec((1, tiles, CAP, GROUP * TILE), lambda k: (k, 0, 0, 0))
    return wide, narrow, folded, like((KVH, tiles, CAP, GROUP * TILE), F32)


def attention_scores(queries, keys):
    wide, narrow, folded, shape = attention_specs(queries.shape[0])
    flops = 2 * queries.size * TILE
    return per_head(scores_kernel, "scores", [wide, narrow], [(shape, folded)], (queries, keys), flops)[0]


def attention_probs(scores, masks, upstream, after):
    slots = upstream.shape[0]
    wide, narrow, folded, shape = attention_specs(slots)
    masks_spec = pl.BlockSpec(masks.shape, lambda k: (0, 0, 0))
    outs = [(like((slots, KVH * HD), BF16), narrow), (shape, folded)]
    flops = 2 * upstream.size * TILE
    return per_head(probs_kernel, "probs", [folded, masks_spec, wide] + [ANY] * len(after), outs, (scores, masks, upstream, *after), flops)


def attention_dscore(probs, values, upstream, queries, keys):
    wide, narrow, folded, _ = attention_specs(queries.shape[0])
    token = (TOKEN, pl.BlockSpec(TOKEN.shape, lambda k: (0, 0)))
    outs = [(like(queries.shape, BF16), wide), (like(keys.shape, BF16), narrow), token]
    args = (probs, values, upstream, queries, keys)
    flops = 6 * upstream.size * TILE
    return per_head(dscore_kernel, "dscore", [folded, narrow, wide, wide, narrow], outs, args, flops)


def slice_of(weights, s):
    half = weights.shape[1] // NZH
    rows = slice(s // NX * half, (s // NX + 1) * half)
    return jnp.concatenate([weights[cr * NX + s % NX, rows] for cr in range(NCO)], axis=0)


def partial_kernel(*refs):
    ins, (v0, v1, v2, v3, x, w, sems) = refs[: NY + SLICES], refs[NY + SLICES :]
    rows, width = x.shape[1], w.shape[1]
    copies = fetch(ins, [x.at[k] for k in range(NY)] + [w.at[i] for i in range(SLICES)], sems)
    for copy in copies:
        copy.wait()
    total = None
    for s in range(SLICES):
        stack = jnp.concatenate([x[k, :, s * width : (s + 1) * width] for k in range(NY)], axis=0)
        term = dot(stack, slice_of(w, s), (1, 0))
        total = term if total is None else total + term
    for k, out in enumerate((v0, v1, v2, v3)):
        out[...] = total[k * rows : (k + 1) * rows].astype(out.dtype)


def staged(*groups):
    stacks = [pltpu.VMEM((len(g), *g[0].shape), g[0].dtype) for g in groups]
    return (*stacks, pltpu.SemaphoreType.DMA((sum(map(len, groups)),)))


def partial_values(pieces, weights):
    rows, width = pieces[0].shape[0], weights[0].shape[1]
    out = [like((rows, width), F32)] + [like((rows, width), BF16)] * (NY - 1)
    flops = 2 * NY * pieces[0].size * width
    ins, scratch = [ANY] * (NY + SLICES), staged(pieces, weights)
    return call(partial_kernel, "partial_values", out, *pieces, *weights, ins=ins, scratch=scratch, mib=56, flops=flops)


def place_kernel(slot, own, a, b, c, after, out):
    rows = own[...] + a[...].astype(F32) + b[...].astype(F32) + c[...].astype(F32)
    at = lax.broadcasted_iota(jnp.int32, (out.shape[0], own.shape[0]), 0)
    chosen = jnp.where(at == slot[...], 1.0, 0.0).astype(BF16)
    out[...] = dot(chosen, rows.astype(BF16), (1, 0)).astype(BF16)


def pick_kernel(*refs):
    slot, buffer, out = refs[0], refs[1], refs[-1]
    at = lax.broadcasted_iota(jnp.int32, (buffer.shape[0], out.shape[0]), 0)
    chosen = jnp.where(at == slot[...], 1.0, 0.0).astype(BF16)
    out[...] = dot(chosen, buffer[...], (0, 0)).astype(BF16)


def back_kernel(*refs):
    ins, (_, g0, g1, g2, g3, r, w, sems) = refs[: NY + SLICES], refs[NY + SLICES :]
    rows, width = r.shape[1], w.shape[1]
    copies = fetch(ins, [r.at[k] for k in range(NY)] + [w.at[i] for i in range(SLICES)], sems)
    for copy in copies:
        copy.wait()
    stack = r[...].reshape(NY * rows, r.shape[2])
    for s in range(SLICES):
        grad = dot(stack, slice_of(w, s), (1, 1)).astype(BF16)
        for k, out in enumerate((g0, g1, g2, g3)):
            out[:, s * width : (s + 1) * width] = grad[k * rows : (k + 1) * rows]


def back(grads, weights, after):
    rows, width = grads[0].shape
    columns = SLICES * weights[0].shape[0]
    flops = 2 * NY * rows * width * columns
    ins, scratch = [ANY] * (NY + SLICES + 1), staged(grads, weights)
    out = [like((rows, columns), BF16)] * NY
    return call(back_kernel, "back", out, *grads, *weights, after, ins=ins, scratch=scratch, mib=56, flops=flops)


def share_kernel(*refs):
    ins, (_, own, other, x, r, sems) = refs[: 2 * NY], refs[2 * NY :]
    half = own.shape[1]
    copies = fetch(ins, [x.at[k] for k in range(NY)] + [r.at[k] for k in range(NY)], sems)
    for copy in copies:
        copy.wait()
    grads = r[...].reshape(NY * r.shape[1], r.shape[2])
    for s in range(SLICES):
        stack = jnp.concatenate([x[k, :, s * NCO * half : (s + 1) * NCO * half] for k in range(NY)], axis=0)
        share = dot(stack, grads, (0, 0))
        own[s] = share[:half]
        other[s] = share[half:].astype(other.dtype)


def shares(pieces, grads, after):
    half, width = pieces[0].shape[1] // SLICES // NCO, grads[0].shape[1]
    shape = (SLICES, half, width)
    flops = 2 * NY * pieces[0].size * width
    out = [like(shape, F32), like(shape, BF16)]
    ins, scratch = [ANY] * (2 * NY + 1), staged(pieces, grads)
    return call(share_kernel, "shares", out, *pieces, *grads, after, ins=ins, scratch=scratch, mib=20, flops=flops)


def core_sum_kernel(own, got, keep, s1, s2, s3):
    for zr in range(NZH):
        for xr, out in enumerate((keep, s1, s2, s3)):
            out[zr] = (own[zr * NX + xr] + got[zr * NX + xr].astype(F32)).astype(out.dtype)


def x_sum_kernel(keep, a, b, c, p1, p2, p3, near, far):
    for zr, out in enumerate((near, far)):
        total = keep[zr] + a[zr].astype(F32) + b[zr].astype(F32) + c[zr].astype(F32)
        out[...] = total.astype(out.dtype)


def stack_kernel(a, b, out):
    rows = a.shape[0]
    out[:rows] = a[...]
    out[rows:] = b[...]


def pair_sum_kernel(*refs):
    a, b, out = refs[0], refs[1], refs[-1]
    out[...] = (a[...].astype(F32) + b[...].astype(F32)).astype(out.dtype)


def halves_kernel(mine, other, out):
    core, rows = at_place()[0], mine.shape[0]
    out[pl.ds(pl.multiple_of(core * rows, rows), rows), :] = mine[...]
    out[pl.ds(pl.multiple_of((1 - core) * rows, rows), rows), :] = other[...]


def body(inputs, value_weight, send_slot, response_id, queries, keys, upstream):
    peers = lax.axis_size("fsdp")
    slots, rows = queries.shape[0], inputs.shape[0]
    half, width = value_weight.shape[0] // NCO, value_weight.shape[1]
    slot = send_slot.reshape(1, rows)

    def exchange(buffer):
        return lax.all_to_all(buffer, "fsdp", split_axis=0, concat_axis=0, tiled=True)

    *pieces, near = split(inputs, value_weight)
    masks = exchange(run_masks(send_slot, response_id, peers, near))
    pieces = [pieces[0]] + [permute(pieces[k], along_y(k)) for k in range(1, NY)]
    pair = call(stack_kernel, "pair", [like((NZH * half, width), BF16)], near, permute(near, mirror))[0]
    weights = [pair] + [permute(pair, along_x(k)) for k in range(1, NX)]
    weights += [permute(weight, other_core) for weight in weights]

    scores = attention_scores(queries, keys)
    grad_v, probs = attention_probs(scores, masks, upstream, (pair, pieces[1], pieces[3]))
    returned = exchange(grad_v)
    after = (pieces[2], *weights[1:NX])
    order, out = [VMEM] * 2 + [ANY] * NX, [like((rows, width), BF16)]
    row_grad = call(pick_kernel, "pick", out, slot, returned, *after, ins=order)[0]
    grads = [row_grad] + [permute(row_grad, along_y(k)) for k in range(1, NY)]

    partial, *parts = partial_values(pieces, weights)
    own, other = shares(pieces, grads, parts[0])
    got = permute(other, other_core)
    out = [like((NZH, half, width), F32)] + [like((NZH, half, width), BF16)] * (NX - 1)
    keep, *sends = call(core_sum_kernel, "core_sum", out, own, got, mib=8)
    arrived = [permute(send, along_x(-k)) for k, send in enumerate(sends, 1)]

    mine, *sends = back(grads, weights, keep)
    parts = [permute(part, along_y(-k)) for k, part in enumerate(parts, 1)]
    columns = [mine] + [permute(send, along_y(-k)) for k, send in enumerate(sends, 1)]

    order, out = [VMEM] * NX + [ANY] * (NY - 1), [like((half, width), F32), like((half, width), BF16)]
    near, far = call(x_sum_kernel, "x_sum", out, keep, *arrived, *parts, ins=order)
    order, out = [VMEM] * 5 + [ANY], [like((slots, width), BF16)]
    value_buffer = call(place_kernel, "place", out, slot, partial, *parts, near, ins=order)[0]
    values = exchange(value_buffer)
    grad_q, grad_k, scored = attention_dscore(probs, values, upstream, queries, keys)
    grad_inputs, joined = join(columns)

    small, order = [like((half, width), BF16)], [VMEM, VMEM, ANY]
    total = call(pair_sum_kernel, "mirror_sum", small, near, permute(far, mirror), scored, ins=order)[0]
    total = call(pair_sum_kernel, "z_sum", small, total, permute(total, flip_zl(1)), joined, ins=order)[0]
    total = call(pair_sum_kernel, "z_sum", small, total, permute(total, flip_zl(2)))[0]
    out = [like((NCO * half, width), BF16)]
    grad_weight = call(halves_kernel, "halves", out, total, permute(total, other_core))[0]
    return grad_inputs, grad_q, grad_k, grad_weight


def solution(mesh):
    spread, sharded = P(("rep", "fsdp"), None), P("fsdp", None)
    line = P(("rep", "fsdp"))
    return jax.shard_map(
        body,
        mesh=mesh,
        in_specs=(spread, sharded, line, line, spread, spread, spread),
        out_specs=(spread, spread, spread, sharded),
        check_vma=False,
    )
```

```python
import jax
import jax.numpy as jnp
from jax import lax
from jax.experimental import pallas as pl
from jax.experimental.pallas import tpu as pltpu
from jax.sharding import PartitionSpec as P

KVH = 4
GROUP = 8
HD = 128
CAP = 8
TILE = 128
BLOCKS = TILE // CAP
AXES = ("rep", "fsdp")
F32 = jnp.float32
BF16 = jnp.bfloat16
NZL, NCO, NZH, NX, NY = 4, 2, 2, 4, 4
SLICES = NZH * NX
TOKEN = jax.ShapeDtypeStruct((8, 128), jnp.float32)
VMEM = pl.BlockSpec(memory_space=pltpu.VMEM)
ANY = pl.BlockSpec(memory_space=pl.ANY)


def permute(array, move):
    pairs = []
    for e in range(NZL * NCO * NZH * NX * NY):
        place = (e // 64, e // 32 % 2, e // 16 % 2, e // 4 % 4, e % 4)
        zl, co, zh, x, y = move(*place)
        pairs.append((e, (((zl * NCO + co) * NZH + zh) * NX + x % NX) * NY + y % NY))
    return lax.ppermute(array, AXES, pairs)


def along_y(k):
    return lambda zl, co, zh, x, y: (zl, co, zh, x, y + k)


def along_x(k):
    return lambda zl, co, zh, x, y: (zl, co, zh, x + k, y)


def other_core(zl, co, zh, x, y):
    return zl, 1 - co, zh, x, y


def mirror(zl, co, zh, x, y):
    return NZL - 1 - zl, co, 1 - zh, x, y


def flip_zl(bit):
    return lambda zl, co, zh, x, y: (zl ^ bit, co, zh, x, y)


def call(kernel, name, out, *args, ins=None, outs=None, scratch=(), mib=4, flops=0):
    size = sum(a.size * a.dtype.itemsize for a in args) + sum(o.size * o.dtype.itemsize for o in out)
    return pl.pallas_call(
        kernel,
        out_shape=out,
        in_specs=[VMEM] * len(args) if ins is None else ins,
        out_specs=[VMEM] * len(out) if outs is None else outs,
        scratch_shapes=scratch,
        compiler_params=pltpu.CompilerParams(vmem_limit_bytes=mib * 1024 * 1024),
        cost_estimate=pl.CostEstimate(flops=flops, bytes_accessed=size, transcendentals=0),
        name=name,
    )(*args)


def fetch(sources, targets, sems):
    copies = [pltpu.make_async_copy(s, t, sems.at[i]) for i, (s, t) in enumerate(zip(sources, targets, strict=True))]
    for copy in copies:
        copy.start()
    return copies


def at_place():
    rep, fsdp = lax.axis_index("rep"), lax.axis_index("fsdp")
    return lax.rem(rep, NCO), lax.div(fsdp, NX * NY), lax.rem(lax.div(fsdp, NY), NX), lax.rem(fsdp, NY)


def like(shape, dtype):
    return jax.ShapeDtypeStruct(shape, dtype)


def dot(a, b, over):
    return lax.dot_general(a, b, (((over[0],), (over[1],)), ((), ())), preferred_element_type=F32)


def feature_blocks(k):
    core, zh, x, y = at_place()
    for zr in range(NZH):
        for xr in range(NX):
            z = zh + zr - 2 * zh * zr
            slice_at = (z * NX + lax.rem(x - xr + NX, NX)) * NY + lax.rem(y + k, NY)
            for cr in range(NCO):
                yield (zr * NX + xr) * NCO + cr, slice_at * NCO + core + cr - 2 * core * cr


def finish(token):
    token[...] = jnp.zeros(token.shape, token.dtype)


def masks_kernel(slots_in, ids_in, masks, slots, ids, sems):
    copies = fetch((slots_in, ids_in), (slots, ids), sems)
    lane = lax.broadcasted_iota(jnp.int32, (CAP, TILE), 1) & (CAP - 1)
    sub = lax.broadcasted_iota(jnp.int32, (CAP, TILE), 0)
    causal = sub <= lane
    plain = causal.astype(jnp.int32)
    for p in range(masks.shape[0]):
        masks[p] = plain
    for copy in copies:
        copy.wait()
    for r in range(slots.shape[0] // CAP):
        keys = jnp.zeros((CAP, TILE), jnp.int32)
        rows = jnp.zeros((CAP, TILE), jnp.int32)
        for j in range(CAP):
            value = ids[r * CAP + j]
            keys = jnp.where(sub == j, value, keys)
            rows = jnp.where(lane == j, value, rows)
        masks[lax.div(slots[r * CAP], CAP)] = jnp.where((keys == rows) & causal, 1, 0)


def run_masks(slots, ids, peers):
    index = pltpu.SMEM(slots.shape, jnp.int32)
    scratch = (index, index, pltpu.SemaphoreType.DMA((2,)))
    out = [like((peers, CAP, TILE), jnp.int32)]
    return call(masks_kernel, "masks", out, slots, ids, ins=[ANY] * 2, scratch=scratch, mib=56)[0]


def split_kernel(full_in, after, p0, p1, p2, p3, full, sems):
    for copy in fetch((full_in,), (full,), sems):
        copy.wait()
    width = full.shape[1] // (NY * SLICES * NCO)
    for k, part in enumerate((p0, p1, p2, p3)):
        for at, block in feature_blocks(k):
            part[:, at * width : (at + 1) * width] = full[:, pl.ds(pl.multiple_of(block * width, width), width)]


def split(full, after):
    rows, columns = full.shape
    out = [like((rows, columns // NY), full.dtype)] * NY
    scratch = (pltpu.VMEM(full.shape, full.dtype), pltpu.SemaphoreType.DMA((1,)))
    return call(split_kernel, "split", out, full, after, ins=[ANY] * 2, scratch=scratch, mib=56)


def join_kernel(p0, p1, p2, p3, full, token):
    finish(token)
    width = p0.shape[1] // (SLICES * NCO)
    for k, part in enumerate((p0, p1, p2, p3)):
        for at, block in feature_blocks(k):
            full[:, pl.ds(pl.multiple_of(block * width, width), width)] = part[:, at * width : (at + 1) * width]


def join(parts):
    rows, columns = parts[0].shape
    return call(join_kernel, "join", [like((rows, columns * NY), parts[0].dtype), TOKEN], *parts, mib=56)


def heads(block, t):
    rows = block[t * TILE : (t + 1) * TILE, :]
    return jnp.concatenate([rows[:, h * HD : (h + 1) * HD] for h in range(GROUP)], axis=0)


def own_block(lanes):
    return lax.broadcasted_iota(jnp.int32, (CAP, lanes), 1) % TILE // CAP


def fold(pairs, block):
    out = pairs[0:CAP]
    for b in range(1, BLOCKS):
        out = jnp.where(block == b, pairs[b * CAP : (b + 1) * CAP], out)
    return out


def unfold(folded, block):
    return jnp.concatenate([jnp.where(block == b, folded, 0.0) for b in range(BLOCKS)], axis=0).astype(BF16)


def head_blocks(array):
    width = GROUP * HD
    return [array.at[:, pl.ds(k * width, width)] for k in range(KVH)]


def scores_kernel(queries, keys_in, scores, q, keys, sems):
    copies = fetch([keys_in] + head_blocks(queries), [keys] + [q.at[k] for k in range(KVH)], sems)
    block = own_block(GROUP * TILE)
    copies[0].wait()
    for k in range(KVH):
        copies[1 + k].wait()
        for t in range(scores.shape[1]):
            pairs = dot(keys[t * TILE : (t + 1) * TILE, k * HD : (k + 1) * HD], heads(q[k], t), (1, 1))
            scores[k, t] = fold(pairs, block)


def probs_kernel(scores_in, masks_in, upstream, *rest):
    grad_v, probs, u, scores, masks, sems = rest[-6:]
    sources = [scores_in, masks_in] + head_blocks(upstream)
    copies = fetch(sources, [scores, masks] + [u.at[k] for k in range(KVH)], sems)
    small, block = own_block(TILE), own_block(GROUP * TILE)
    copies[0].wait()
    copies[1].wait()
    seen = []
    for t in range(scores.shape[1]):
        mask = masks[t * BLOCKS]
        for b in range(1, BLOCKS):
            mask = jnp.where(small == b, masks[t * BLOCKS + b], mask)
        seen.append(jnp.concatenate([mask] * GROUP, axis=1) != 0)
    for k in range(KVH):
        copies[2 + k].wait()
        for t, visible in enumerate(seen):
            masked = jnp.where(visible, scores[k, t] * (1.0 / HD**0.5), -1e30)
            top = jnp.max(masked, axis=0, keepdims=True)
            expo = jnp.where(visible, jnp.exp(masked - top), 0.0)
            prob = expo / jnp.sum(expo, axis=0, keepdims=True)
            probs[k, t] = prob
            grad = dot(unfold(prob, block), heads(u[k], t), (1, 0))
            grad_v[t * TILE : (t + 1) * TILE, k * HD : (k + 1) * HD] = grad.astype(BF16)


def dscore_kernel(probs, values, upstream, queries, keys, grad_q, grad_k, token):
    finish(token)
    scale = 1.0 / HD**0.5
    block = own_block(GROUP * TILE)
    for t in range(probs.shape[1]):
        rows = slice(t * TILE, (t + 1) * TILE)
        prob = probs[0, t]
        dprob = fold(dot(values[rows, :], heads(upstream, t), (1, 1)), block)
        delta = jnp.sum(prob * dprob, axis=0, keepdims=True)
        dscore = unfold(prob * (dprob - delta), block)
        grad_k[rows, :] = (dot(dscore, heads(queries, t), (1, 0)) * scale).astype(BF16)
        grad = (dot(dscore, keys[rows, :], (0, 0)) * scale).astype(BF16)
        for h in range(GROUP):
            grad_q[rows, h * HD : (h + 1) * HD] = grad[h * TILE : (h + 1) * TILE]


def per_head(kernel, name, ins, outs, args, flops):
    size = sum(a.size * a.dtype.itemsize for a in args) + sum(o.size * o.dtype.itemsize for o, _ in outs)
    return pl.pallas_call(
        kernel,
        grid=(KVH,),
        out_shape=[o for o, _ in outs],
        in_specs=ins,
        out_specs=[s for _, s in outs],
        compiler_params=pltpu.CompilerParams(vmem_limit_bytes=56 * 1024 * 1024),
        cost_estimate=pl.CostEstimate(flops=flops, bytes_accessed=size, transcendentals=0),
        name=name,
    )(*args)


def attention_specs(slots):
    wide = pl.BlockSpec((slots, GROUP * HD), lambda k: (0, k))
    narrow = pl.BlockSpec((slots, HD), lambda k: (0, k))
    tiles = slots // TILE
    folded = pl.BlockSpec((1, tiles, CAP, GROUP * TILE), lambda k: (k, 0, 0, 0))
    return wide, narrow, folded, like((KVH, tiles, CAP, GROUP * TILE), F32)


def folded_shape(slots):
    return (KVH, slots // TILE, CAP, GROUP * TILE)


def attention_scores(queries, keys):
    slots = queries.shape[0]
    sems = pltpu.SemaphoreType.DMA((1 + KVH,))
    scratch = (pltpu.VMEM((KVH, slots, GROUP * HD), BF16), pltpu.VMEM(keys.shape, BF16), sems)
    out = [like(folded_shape(slots), F32)]
    flops = 2 * queries.size * TILE
    return call(scores_kernel, "scores", out, queries, keys, ins=[ANY] * 2, scratch=scratch, mib=56, flops=flops)[0]


def attention_probs(scores, masks, upstream, after):
    slots = upstream.shape[0]
    u = pltpu.VMEM((KVH, slots, GROUP * HD), BF16)
    sems = pltpu.SemaphoreType.DMA((2 + KVH,))
    scratch = (u, pltpu.VMEM(scores.shape, F32), pltpu.VMEM(masks.shape, jnp.int32), sems)
    out = [like((slots, KVH * HD), BF16), like(scores.shape, F32)]
    flops = 2 * upstream.size * TILE
    ins = [ANY] * (3 + len(after))
    return call(probs_kernel, "probs", out, scores, masks, upstream, *after, ins=ins, scratch=scratch, mib=56, flops=flops)


def attention_dscore(probs, values, upstream, queries, keys):
    wide, narrow, folded, _ = attention_specs(queries.shape[0])
    token = (TOKEN, pl.BlockSpec(TOKEN.shape, lambda k: (0, 0)))
    outs = [(like(queries.shape, BF16), wide), (like(keys.shape, BF16), narrow), token]
    args = (probs, values, upstream, queries, keys)
    flops = 6 * upstream.size * TILE
    return per_head(dscore_kernel, "dscore", [folded, narrow, wide, wide, narrow], outs, args, flops)


def slice_of(weights, s):
    half = weights.shape[1] // NZH
    rows = slice(s // NX * half, (s // NX + 1) * half)
    return jnp.concatenate([weights[cr * NX + s % NX, rows] for cr in range(NCO)], axis=0)


def partial_kernel(*refs):
    ins, (_, v0, v1, v2, v3, x, w, sems) = refs[: NY + SLICES], refs[NY + SLICES :]
    rows, width = x.shape[1], w.shape[1]
    copies = fetch(ins, [x.at[k] for k in range(NY)] + [w.at[i] for i in range(SLICES)], sems)
    for copy in copies:
        copy.wait()
    total = None
    for s in range(SLICES):
        stack = jnp.concatenate([x[k, :, s * width : (s + 1) * width] for k in range(NY)], axis=0)
        term = dot(stack, slice_of(w, s), (1, 0))
        total = term if total is None else total + term
    for k, out in enumerate((v0, v1, v2, v3)):
        out[...] = total[k * rows : (k + 1) * rows].astype(out.dtype)


def staged(*groups):
    stacks = [pltpu.VMEM((len(g), *g[0].shape), g[0].dtype) for g in groups]
    return (*stacks, pltpu.SemaphoreType.DMA((sum(map(len, groups)),)))


def partial_values(pieces, weights, after):
    rows, width = pieces[0].shape[0], weights[0].shape[1]
    out = [like((rows, width), F32)] + [like((rows, width), BF16)] * (NY - 1)
    flops = 2 * NY * pieces[0].size * width
    ins, scratch = [ANY] * (NY + SLICES + 1), staged(pieces, weights)
    return call(partial_kernel, "partial_values", out, *pieces, *weights, after, ins=ins, scratch=scratch, mib=56, flops=flops)


def place_kernel(slot, own, a, b, c, after, out):
    rows = own[...] + a[...].astype(F32) + b[...].astype(F32) + c[...].astype(F32)
    at = lax.broadcasted_iota(jnp.int32, (out.shape[0], own.shape[0]), 0)
    chosen = jnp.where(at == slot[...], 1.0, 0.0).astype(BF16)
    out[...] = dot(chosen, rows.astype(BF16), (1, 0)).astype(BF16)


def pick_kernel(*refs):
    slot, buffer, out = refs[0], refs[1], refs[-1]
    at = lax.broadcasted_iota(jnp.int32, (buffer.shape[0], out.shape[0]), 0)
    chosen = jnp.where(at == slot[...], 1.0, 0.0).astype(BF16)
    out[...] = dot(chosen, buffer[...], (0, 0)).astype(BF16)


def back_kernel(*refs):
    ins, (_, g0, g1, g2, g3, token, r, w, sems) = refs[: NY + SLICES], refs[NY + SLICES :]
    finish(token)
    rows, width = r.shape[1], w.shape[1]
    copies = fetch(ins, [r.at[k] for k in range(NY)] + [w.at[i] for i in range(SLICES)], sems)
    for copy in copies:
        copy.wait()
    stack = r[...].reshape(NY * rows, r.shape[2])
    for s in range(SLICES):
        grad = dot(stack, slice_of(w, s), (1, 1)).astype(BF16)
        for k, out in enumerate((g0, g1, g2, g3)):
            out[:, s * width : (s + 1) * width] = grad[k * rows : (k + 1) * rows]


def back(grads, weights, after):
    rows, width = grads[0].shape
    columns = SLICES * weights[0].shape[0]
    flops = 2 * NY * rows * width * columns
    ins, scratch = [ANY] * (NY + SLICES + 1), staged(grads, weights)
    out = [like((rows, columns), BF16)] * NY + [TOKEN]
    return call(back_kernel, "back", out, *grads, *weights, after, ins=ins, scratch=scratch, mib=56, flops=flops)


def share_kernel(*refs):
    ins, (own, other, token, x, r, sems) = refs[: 2 * NY], refs[-6:]
    finish(token)
    half = own.shape[1]
    copies = fetch(ins, [x.at[k] for k in range(NY)] + [r.at[k] for k in range(NY)], sems)
    for copy in copies:
        copy.wait()
    grads = r[...].reshape(NY * r.shape[1], r.shape[2])
    for s in range(SLICES):
        stack = jnp.concatenate([x[k, :, s * NCO * half : (s + 1) * NCO * half] for k in range(NY)], axis=0)
        share = dot(stack, grads, (0, 0))
        own[s] = share[:half]
        other[s] = share[half:].astype(other.dtype)


def shares(pieces, grads, after):
    half, width = pieces[0].shape[1] // SLICES // NCO, grads[0].shape[1]
    shape = (SLICES, half, width)
    flops = 2 * NY * pieces[0].size * width
    out = [like(shape, F32), like(shape, BF16), TOKEN]
    ins, scratch = [ANY] * (2 * NY + len(after)), staged(pieces, grads)
    return call(share_kernel, "shares", out, *pieces, *grads, *after, ins=ins, scratch=scratch, mib=20, flops=flops)


def core_sum_kernel(own, got, keep, s1, s2, s3):
    for zr in range(NZH):
        for xr, out in enumerate((keep, s1, s2, s3)):
            out[zr] = (own[zr * NX + xr] + got[zr * NX + xr].astype(F32)).astype(out.dtype)


def x_sum_kernel(keep, a, b, c, after, near, far):
    for zr, out in enumerate((near, far)):
        total = keep[zr] + a[zr].astype(F32) + b[zr].astype(F32) + c[zr].astype(F32)
        out[...] = total.astype(out.dtype)


def stack_kernel(a, b, out):
    rows = a.shape[0] // NCO
    here = pl.ds(pl.multiple_of(at_place()[0] * rows, rows), rows)
    out[:rows] = a[here, :]
    out[rows:] = b[here, :]


def pair_sum_kernel(*refs):
    a, b, out = refs[0], refs[1], refs[-1]
    out[...] = (a[...].astype(F32) + b[...].astype(F32)).astype(out.dtype)


def halves_kernel(mine, other, after, out):
    core, rows = at_place()[0], mine.shape[0]
    out[pl.ds(pl.multiple_of(core * rows, rows), rows), :] = mine[...]
    out[pl.ds(pl.multiple_of((1 - core) * rows, rows), rows), :] = other[...]


def body(inputs, value_weight, send_slot, response_id, queries, keys, upstream):
    peers = lax.axis_size("fsdp")
    slots, rows = queries.shape[0], inputs.shape[0]
    half, width = value_weight.shape[0] // NCO, value_weight.shape[1]
    slot = send_slot.reshape(1, rows)

    def exchange(buffer):
        return lax.all_to_all(buffer, "fsdp", split_axis=0, concat_axis=0, tiled=True)

    mask = run_masks(send_slot, response_id, peers)
    masks = exchange(mask)
    mirrored = permute(value_weight, mirror)
    pieces = split(inputs, mask)
    pieces = [pieces[0]] + [permute(pieces[k], along_y(k)) for k in range(1, NY)]
    pair = call(stack_kernel, "pair", [like((NZH * half, width), BF16)], value_weight, mirrored)[0]
    weights = [pair] + [permute(pair, along_x(k)) for k in range(1, NX)]
    weights += [permute(weight, other_core) for weight in weights]

    scores = attention_scores(queries, keys)
    grad_v, probs = attention_probs(scores, masks, upstream, (pair,))
    returned = exchange(grad_v)
    order, out = [VMEM] * 2 + [ANY] * (NY - 1), [like((rows, width), BF16)]
    row_grad = call(pick_kernel, "pick", out, slot, returned, *pieces[1:], ins=order)[0]
    grads = [row_grad] + [permute(row_grad, along_y(k)) for k in range(1, NY)]

    own, other, shared = shares(pieces, grads, weights[1:NX])
    partial, *parts = partial_values(pieces, weights, shared)
    parts = [permute(part, along_y(-k)) for k, part in enumerate(parts, 1)]
    got = permute(other, other_core)
    out = [like((NZH, half, width), F32)] + [like((NZH, half, width), BF16)] * (NX - 1)
    keep, *sends = call(core_sum_kernel, "core_sum", out, own, got, mib=8)
    arrived = [permute(send, along_x(-k)) for k, send in enumerate(sends, 1)]

    mine, *sends, backed = back(grads, weights, keep)
    columns = [mine] + [permute(send, along_y(-k)) for k, send in enumerate(sends, 1)]

    out = [like((half, width), F32), like((half, width), BF16)]
    near, far = call(x_sum_kernel, "x_sum", out, keep, *arrived, backed, ins=[VMEM] * NX + [ANY])
    small, order = [like((half, width), BF16)], [VMEM, VMEM, ANY]
    total = call(pair_sum_kernel, "mirror_sum", small, near, permute(far, mirror), *parts, ins=[VMEM] * 2 + [ANY] * (NY - 1))[0]

    after, out = [VMEM] * 5 + [ANY], [like((slots, width), BF16)]
    value_buffer = call(place_kernel, "place", out, slot, partial, *parts, total, ins=after)[0]
    values = exchange(value_buffer)
    grad_q, grad_k, scored = attention_dscore(probs, values, upstream, queries, keys)
    grad_inputs, joined = join(columns)

    after = [VMEM] * 2 + [ANY] * NY
    total = call(pair_sum_kernel, "z_sum", small, total, permute(total, flip_zl(1)), scored, *columns[1:], ins=after)[0]
    total = call(pair_sum_kernel, "z_sum", small, total, permute(total, flip_zl(2)))[0]
    out = [like((NCO * half, width), BF16)]
    grad_weight = call(halves_kernel, "halves", out, total, permute(total, other_core), joined, ins=order)[0]
    return grad_inputs, grad_q, grad_k, grad_weight


def solution(mesh):
    spread, sharded = P(("rep", "fsdp"), None), P("fsdp", None)
    line = P(("rep", "fsdp"))
    return jax.shard_map(
        body,
        mesh=mesh,
        in_specs=(spread, sharded, line, line, spread, spread, spread),
        out_specs=(spread, spread, spread, sharded),
        check_vma=False,
    )
```

```python
import jax
import jax.numpy as jnp
from jax import lax
from jax.experimental import pallas as pl
from jax.experimental.pallas import tpu as pltpu
from jax.sharding import PartitionSpec as P

KVH = 4
GROUP = 8
HD = 128
CAP = 8
TILE = 128
BLOCKS = TILE // CAP
AXES = ("rep", "fsdp")
F32 = jnp.float32
BF16 = jnp.bfloat16
NZL, NCO, NZH, NX, NY = 4, 2, 2, 4, 4
SLICES = NZH * NX
TOKEN = jax.ShapeDtypeStruct((8, 128), jnp.float32)
VMEM = pl.BlockSpec(memory_space=pltpu.VMEM)
ANY = pl.BlockSpec(memory_space=pl.ANY)


def permute(array, move):
    pairs = []
    for e in range(NZL * NCO * NZH * NX * NY):
        place = (e // 64, e // 32 % 2, e // 16 % 2, e // 4 % 4, e % 4)
        zl, co, zh, x, y = move(*place)
        pairs.append((e, (((zl * NCO + co) * NZH + zh) * NX + x % NX) * NY + y % NY))
    return lax.ppermute(array, AXES, pairs)


def along_y(k):
    return lambda zl, co, zh, x, y: (zl, co, zh, x, y + k)


def along_x(k):
    return lambda zl, co, zh, x, y: (zl, co, zh, x + k, y)


def other_core(zl, co, zh, x, y):
    return zl, 1 - co, zh, x, y


def mirror(zl, co, zh, x, y):
    return NZL - 1 - zl, co, 1 - zh, x, y


def flip_zl(bit):
    return lambda zl, co, zh, x, y: (zl ^ bit, co, zh, x, y)


def call(kernel, name, out, *args, ins=None, outs=None, scratch=(), mib=4, flops=0):
    size = sum(a.size * a.dtype.itemsize for a in args) + sum(o.size * o.dtype.itemsize for o in out)
    return pl.pallas_call(
        kernel,
        out_shape=out,
        in_specs=[VMEM] * len(args) if ins is None else ins,
        out_specs=[VMEM] * len(out) if outs is None else outs,
        scratch_shapes=scratch,
        compiler_params=pltpu.CompilerParams(vmem_limit_bytes=mib * 1024 * 1024),
        cost_estimate=pl.CostEstimate(flops=flops, bytes_accessed=size, transcendentals=0),
        name=name,
    )(*args)


def fetch(sources, targets, sems):
    copies = [pltpu.make_async_copy(s, t, sems.at[i]) for i, (s, t) in enumerate(zip(sources, targets, strict=True))]
    for copy in copies:
        copy.start()
    return copies


def at_place():
    rep, fsdp = lax.axis_index("rep"), lax.axis_index("fsdp")
    return lax.rem(rep, NCO), lax.div(fsdp, NX * NY), lax.rem(lax.div(fsdp, NY), NX), lax.rem(fsdp, NY)


def like(shape, dtype):
    return jax.ShapeDtypeStruct(shape, dtype)


def dot(a, b, over):
    return lax.dot_general(a, b, (((over[0],), (over[1],)), ((), ())), preferred_element_type=F32)


def feature_blocks(k):
    core, zh, x, y = at_place()
    for zr in range(NZH):
        for xr in range(NX):
            z = zh + zr - 2 * zh * zr
            slice_at = (z * NX + lax.rem(x - xr + NX, NX)) * NY + lax.rem(y + k, NY)
            for cr in range(NCO):
                yield (zr * NX + xr) * NCO + cr, slice_at * NCO + core + cr - 2 * core * cr


def finish(token):
    token[...] = jnp.zeros(token.shape, token.dtype)


def masks_kernel(slots_in, ids_in, masks, slots, ids, sems):
    copies = fetch((slots_in, ids_in), (slots, ids), sems)
    lane = lax.broadcasted_iota(jnp.int32, (CAP, TILE), 1) & (CAP - 1)
    sub = lax.broadcasted_iota(jnp.int32, (CAP, TILE), 0)
    causal = sub <= lane
    plain = causal.astype(jnp.int32)
    for p in range(masks.shape[0]):
        masks[p] = plain
    for copy in copies:
        copy.wait()
    for r in range(slots.shape[0] // CAP):
        keys = jnp.zeros((CAP, TILE), jnp.int32)
        rows = jnp.zeros((CAP, TILE), jnp.int32)
        for j in range(CAP):
            value = ids[r * CAP + j]
            keys = jnp.where(sub == j, value, keys)
            rows = jnp.where(lane == j, value, rows)
        masks[lax.div(slots[r * CAP], CAP)] = jnp.where((keys == rows) & causal, 1, 0)


def run_masks(slots, ids, peers):
    index = pltpu.SMEM(slots.shape, jnp.int32)
    scratch = (index, index, pltpu.SemaphoreType.DMA((2,)))
    out = [like((peers, CAP, TILE), jnp.int32)]
    return call(masks_kernel, "masks", out, slots, ids, ins=[ANY] * 2, scratch=scratch, mib=56)[0]


def split_kernel(full_in, after, p0, p1, p2, p3, full, sems):
    for copy in fetch((full_in,), (full,), sems):
        copy.wait()
    width = full.shape[1] // (NY * SLICES * NCO)
    for k, part in enumerate((p0, p1, p2, p3)):
        for at, block in feature_blocks(k):
            part[:, at * width : (at + 1) * width] = full[:, pl.ds(pl.multiple_of(block * width, width), width)]


def split(full, after):
    rows, columns = full.shape
    out = [like((rows, columns // NY), full.dtype)] * NY
    scratch = (pltpu.VMEM(full.shape, full.dtype), pltpu.SemaphoreType.DMA((1,)))
    return call(split_kernel, "split", out, full, after, ins=[ANY] * 2, scratch=scratch, mib=56)


def join_kernel(p0, p1, p2, p3, full, token):
    finish(token)
    width = p0.shape[1] // (SLICES * NCO)
    for k, part in enumerate((p0, p1, p2, p3)):
        for at, block in feature_blocks(k):
            full[:, pl.ds(pl.multiple_of(block * width, width), width)] = part[:, at * width : (at + 1) * width]


def join(parts):
    rows, columns = parts[0].shape
    return call(join_kernel, "join", [like((rows, columns * NY), parts[0].dtype), TOKEN], *parts, mib=56)


def heads(block, t):
    rows = block[t * TILE : (t + 1) * TILE, :]
    return jnp.concatenate([rows[:, h * HD : (h + 1) * HD] for h in range(GROUP)], axis=0)


def own_block(lanes):
    return lax.broadcasted_iota(jnp.int32, (CAP, lanes), 1) % TILE // CAP


def fold(pairs, block):
    out = pairs[0:CAP]
    for b in range(1, BLOCKS):
        out = jnp.where(block == b, pairs[b * CAP : (b + 1) * CAP], out)
    return out


def unfold(folded, block):
    return jnp.concatenate([jnp.where(block == b, folded, 0.0) for b in range(BLOCKS)], axis=0).astype(BF16)


def head_blocks(array):
    width = GROUP * HD
    return [array.at[:, pl.ds(k * width, width)] for k in range(KVH)]


def scores_kernel(queries, keys_in, scores, q, keys, sems):
    copies = fetch([keys_in] + head_blocks(queries), [keys] + [q.at[k] for k in range(KVH)], sems)
    block = own_block(GROUP * TILE)
    copies[0].wait()
    for k in range(KVH):
        copies[1 + k].wait()
        for t in range(scores.shape[1]):
            pairs = dot(keys[t * TILE : (t + 1) * TILE, k * HD : (k + 1) * HD], heads(q[k], t), (1, 1))
            scores[k, t] = fold(pairs, block)


def probs_kernel(scores_in, masks_in, upstream, *rest):
    grad_v, probs, u, scores, masks, sems = rest[-6:]
    sources = [scores_in, masks_in] + head_blocks(upstream)
    copies = fetch(sources, [scores, masks] + [u.at[k] for k in range(KVH)], sems)
    small, block = own_block(TILE), own_block(GROUP * TILE)
    copies[0].wait()
    copies[1].wait()
    seen = []
    for t in range(scores.shape[1]):
        mask = masks[t * BLOCKS]
        for b in range(1, BLOCKS):
            mask = jnp.where(small == b, masks[t * BLOCKS + b], mask)
        seen.append(jnp.concatenate([mask] * GROUP, axis=1) != 0)
    for k in range(KVH):
        copies[2 + k].wait()
        for t, visible in enumerate(seen):
            masked = jnp.where(visible, scores[k, t] * (1.0 / HD**0.5), -1e30)
            top = jnp.max(masked, axis=0, keepdims=True)
            expo = jnp.where(visible, jnp.exp(masked - top), 0.0)
            prob = expo / jnp.sum(expo, axis=0, keepdims=True)
            probs[k, t] = prob
            grad = dot(unfold(prob, block), heads(u[k], t), (1, 0))
            grad_v[t * TILE : (t + 1) * TILE, k * HD : (k + 1) * HD] = grad.astype(BF16)


def dscore_kernel(probs, values, upstream, queries, keys, grad_q, grad_k, token):
    finish(token)
    scale = 1.0 / HD**0.5
    block = own_block(GROUP * TILE)
    for t in range(probs.shape[1]):
        rows = slice(t * TILE, (t + 1) * TILE)
        prob = probs[0, t]
        dprob = fold(dot(values[rows, :], heads(upstream, t), (1, 1)), block)
        delta = jnp.sum(prob * dprob, axis=0, keepdims=True)
        dscore = unfold(prob * (dprob - delta), block)
        grad_k[rows, :] = (dot(dscore, heads(queries, t), (1, 0)) * scale).astype(BF16)
        grad = (dot(dscore, keys[rows, :], (0, 0)) * scale).astype(BF16)
        for h in range(GROUP):
            grad_q[rows, h * HD : (h + 1) * HD] = grad[h * TILE : (h + 1) * TILE]


def per_head(kernel, name, ins, outs, args, flops):
    size = sum(a.size * a.dtype.itemsize for a in args) + sum(o.size * o.dtype.itemsize for o, _ in outs)
    return pl.pallas_call(
        kernel,
        grid=(KVH,),
        out_shape=[o for o, _ in outs],
        in_specs=ins,
        out_specs=[s for _, s in outs],
        compiler_params=pltpu.CompilerParams(vmem_limit_bytes=56 * 1024 * 1024),
        cost_estimate=pl.CostEstimate(flops=flops, bytes_accessed=size, transcendentals=0),
        name=name,
    )(*args)


def attention_specs(slots):
    wide = pl.BlockSpec((slots, GROUP * HD), lambda k: (0, k))
    narrow = pl.BlockSpec((slots, HD), lambda k: (0, k))
    tiles = slots // TILE
    folded = pl.BlockSpec((1, tiles, CAP, GROUP * TILE), lambda k: (k, 0, 0, 0))
    return wide, narrow, folded, like((KVH, tiles, CAP, GROUP * TILE), F32)


def folded_shape(slots):
    return (KVH, slots // TILE, CAP, GROUP * TILE)


def attention_scores(queries, keys):
    slots = queries.shape[0]
    sems = pltpu.SemaphoreType.DMA((1 + KVH,))
    scratch = (pltpu.VMEM((KVH, slots, GROUP * HD), BF16), pltpu.VMEM(keys.shape, BF16), sems)
    out = [like(folded_shape(slots), F32)]
    flops = 2 * queries.size * TILE
    return call(scores_kernel, "scores", out, queries, keys, ins=[ANY] * 2, scratch=scratch, mib=56, flops=flops)[0]


def attention_probs(scores, masks, upstream, after):
    slots = upstream.shape[0]
    u = pltpu.VMEM((KVH, slots, GROUP * HD), BF16)
    sems = pltpu.SemaphoreType.DMA((2 + KVH,))
    scratch = (u, pltpu.VMEM(scores.shape, F32), pltpu.VMEM(masks.shape, jnp.int32), sems)
    out = [like((slots, KVH * HD), BF16), like(scores.shape, F32)]
    flops = 2 * upstream.size * TILE
    ins = [ANY] * (3 + len(after))
    return call(probs_kernel, "probs", out, scores, masks, upstream, *after, ins=ins, scratch=scratch, mib=56, flops=flops)


def attention_dscore(probs, values, upstream, queries, keys):
    wide, narrow, folded, _ = attention_specs(queries.shape[0])
    token = (TOKEN, pl.BlockSpec(TOKEN.shape, lambda k: (0, 0)))
    outs = [(like(queries.shape, BF16), wide), (like(keys.shape, BF16), narrow), token]
    args = (probs, values, upstream, queries, keys)
    flops = 6 * upstream.size * TILE
    return per_head(dscore_kernel, "dscore", [folded, narrow, wide, wide, narrow], outs, args, flops)


def slice_of(weights, s):
    half = weights.shape[1] // NZH
    rows = slice(s // NX * half, (s // NX + 1) * half)
    return jnp.concatenate([weights[cr * NX + s % NX, rows] for cr in range(NCO)], axis=0)


def partial_kernel(*refs):
    ins, (_, v0, v1, v2, v3, x, w, sems) = refs[: NY + SLICES], refs[NY + SLICES :]
    rows, width = x.shape[1], w.shape[1]
    copies = fetch(ins, [x.at[k] for k in range(NY)] + [w.at[i] for i in range(SLICES)], sems)
    for copy in copies:
        copy.wait()
    total = None
    for s in range(SLICES):
        stack = jnp.concatenate([x[k, :, s * width : (s + 1) * width] for k in range(NY)], axis=0)
        term = dot(stack, slice_of(w, s), (1, 0))
        total = term if total is None else total + term
    for k, out in enumerate((v0, v1, v2, v3)):
        out[...] = total[k * rows : (k + 1) * rows].astype(out.dtype)


def staged(*groups):
    stacks = [pltpu.VMEM((len(g), *g[0].shape), g[0].dtype) for g in groups]
    return (*stacks, pltpu.SemaphoreType.DMA((sum(map(len, groups)),)))


def partial_values(pieces, weights, after):
    rows, width = pieces[0].shape[0], weights[0].shape[1]
    out = [like((rows, width), F32)] + [like((rows, width), BF16)] * (NY - 1)
    flops = 2 * NY * pieces[0].size * width
    ins, scratch = [ANY] * (NY + SLICES + 1), staged(pieces, weights)
    return call(partial_kernel, "partial_values", out, *pieces, *weights, after, ins=ins, scratch=scratch, mib=56, flops=flops)


def place_kernel(slot, own, a, b, c, after, out):
    rows = own[...] + a[...].astype(F32) + b[...].astype(F32) + c[...].astype(F32)
    at = lax.broadcasted_iota(jnp.int32, (out.shape[0], own.shape[0]), 0)
    chosen = jnp.where(at == slot[...], 1.0, 0.0).astype(BF16)
    out[...] = dot(chosen, rows.astype(BF16), (1, 0)).astype(BF16)


def pick_kernel(*refs):
    slot, buffer, out = refs[0], refs[1], refs[-1]
    at = lax.broadcasted_iota(jnp.int32, (buffer.shape[0], out.shape[0]), 0)
    chosen = jnp.where(at == slot[...], 1.0, 0.0).astype(BF16)
    out[...] = dot(chosen, buffer[...], (0, 0)).astype(BF16)


def back_kernel(*refs):
    ins, (_, g0, g1, g2, g3, token, r, w, sems) = refs[: NY + SLICES], refs[NY + SLICES :]
    finish(token)
    rows, width = r.shape[1], w.shape[1]
    copies = fetch(ins, [r.at[k] for k in range(NY)] + [w.at[i] for i in range(SLICES)], sems)
    for copy in copies:
        copy.wait()
    stack = r[...].reshape(NY * rows, r.shape[2])
    for s in range(SLICES):
        grad = dot(stack, slice_of(w, s), (1, 1)).astype(BF16)
        for k, out in enumerate((g0, g1, g2, g3)):
            out[:, s * width : (s + 1) * width] = grad[k * rows : (k + 1) * rows]


def back(grads, weights, after):
    rows, width = grads[0].shape
    columns = SLICES * weights[0].shape[0]
    flops = 2 * NY * rows * width * columns
    ins, scratch = [ANY] * (NY + SLICES + 1), staged(grads, weights)
    out = [like((rows, columns), BF16)] * NY + [TOKEN]
    return call(back_kernel, "back", out, *grads, *weights, after, ins=ins, scratch=scratch, mib=56, flops=flops)


def share_kernel(*refs):
    ins, (own, other, token, x, r, sems) = refs[: 2 * NY], refs[-6:]
    finish(token)
    half = own.shape[1]
    copies = fetch(ins, [x.at[k] for k in range(NY)] + [r.at[k] for k in range(NY)], sems)
    for copy in copies:
        copy.wait()
    grads = r[...].reshape(NY * r.shape[1], r.shape[2])
    for s in range(SLICES):
        stack = jnp.concatenate([x[k, :, s * NCO * half : (s + 1) * NCO * half] for k in range(NY)], axis=0)
        share = dot(stack, grads, (0, 0))
        own[s] = share[:half]
        other[s] = share[half:].astype(other.dtype)


def shares(pieces, grads, after):
    half, width = pieces[0].shape[1] // SLICES // NCO, grads[0].shape[1]
    shape = (SLICES, half, width)
    flops = 2 * NY * pieces[0].size * width
    out = [like(shape, F32), like(shape, BF16), TOKEN]
    ins, scratch = [ANY] * (2 * NY + len(after)), staged(pieces, grads)
    return call(share_kernel, "shares", out, *pieces, *grads, *after, ins=ins, scratch=scratch, mib=20, flops=flops)


def core_sum_kernel(own, got, keep, s1, s2, s3):
    for zr in range(NZH):
        for xr, out in enumerate((keep, s1, s2, s3)):
            out[zr] = (own[zr * NX + xr] + got[zr * NX + xr].astype(F32)).astype(out.dtype)


def x_sum_kernel(keep, a, b, c, after, near, far):
    for zr, out in enumerate((near, far)):
        total = keep[zr] + a[zr].astype(F32) + b[zr].astype(F32) + c[zr].astype(F32)
        out[...] = total.astype(out.dtype)


def stack_kernel(a, b, out):
    rows = a.shape[0] // NCO
    here = pl.ds(pl.multiple_of(at_place()[0] * rows, rows), rows)
    out[:rows] = a[here, :]
    out[rows:] = b[here, :]


def pair_sum_kernel(*refs):
    a, b, out = refs[0], refs[1], refs[-1]
    out[...] = (a[...].astype(F32) + b[...].astype(F32)).astype(out.dtype)


def halves_kernel(mine, other, after, out):
    core, rows = at_place()[0], mine.shape[0]
    out[pl.ds(pl.multiple_of(core * rows, rows), rows), :] = mine[...]
    out[pl.ds(pl.multiple_of((1 - core) * rows, rows), rows), :] = other[...]


def body(inputs, value_weight, send_slot, response_id, queries, keys, upstream):
    peers = lax.axis_size("fsdp")
    slots, rows = queries.shape[0], inputs.shape[0]
    half, width = value_weight.shape[0] // NCO, value_weight.shape[1]
    slot = send_slot.reshape(1, rows)

    def exchange(buffer):
        return lax.all_to_all(buffer, "fsdp", split_axis=0, concat_axis=0, tiled=True)

    mask = run_masks(send_slot, response_id, peers)
    masks = exchange(mask)
    mirrored = permute(value_weight, mirror)
    pieces = split(inputs, mask)
    pieces = [pieces[0]] + [permute(pieces[k], along_y(k)) for k in range(1, NY)]
    pair = call(stack_kernel, "pair", [like((NZH * half, width), BF16)], value_weight, mirrored)[0]
    weights = [pair] + [permute(pair, along_x(k)) for k in range(1, NX)]
    weights += [permute(weight, other_core) for weight in weights]

    scores = attention_scores(queries, keys)
    grad_v, probs = attention_probs(scores, masks, upstream, (pair,))
    returned = exchange(grad_v)
    order, out = [VMEM] * 2 + [ANY] * (NY - 1), [like((rows, width), BF16)]
    row_grad = call(pick_kernel, "pick", out, slot, returned, *pieces[1:], ins=order)[0]
    grads = [row_grad] + [permute(row_grad, along_y(k)) for k in range(1, NY)]

    own, other, shared = shares(pieces, grads, weights[1:NX])
    partial, *parts = partial_values(pieces, weights, shared)
    parts = [permute(part, along_y(-k)) for k, part in enumerate(parts, 1)]
    got = permute(other, other_core)
    out = [like((NZH, half, width), F32)] + [like((NZH, half, width), BF16)] * (NX - 1)
    keep, *sends = call(core_sum_kernel, "core_sum", out, own, got, mib=8)
    arrived = [permute(send, along_x(-k)) for k, send in enumerate(sends, 1)]

    mine, *sends, backed = back(grads, weights, keep)
    columns = [mine] + [permute(send, along_y(-k)) for k, send in enumerate(sends, 1)]

    out = [like((half, width), F32), like((half, width), BF16)]
    near, far = call(x_sum_kernel, "x_sum", out, keep, *arrived, backed, ins=[VMEM] * NX + [ANY])
    small, order = [like((half, width), BF16)], [VMEM, VMEM, ANY]
    total = call(pair_sum_kernel, "mirror_sum", small, near, permute(far, mirror), *parts, ins=[VMEM] * 2 + [ANY] * (NY - 1))[0]

    after, out = [VMEM] * 5 + [ANY], [like((slots, width), BF16)]
    value_buffer = call(place_kernel, "place", out, slot, partial, *parts, total, ins=after)[0]
    values = exchange(value_buffer)
    grad_q, grad_k, scored = attention_dscore(probs, values, upstream, queries, keys)
    grad_inputs, joined = join(columns)

    after = [VMEM] * 2 + [ANY] * (NY - 1)
    total = call(pair_sum_kernel, "z_sum", small, total, permute(total, flip_zl(1)), *columns[1:], ins=after)[0]
    total = call(pair_sum_kernel, "z_sum", small, total, permute(total, flip_zl(2)), scored, ins=order)[0]
    out = [like((NCO * half, width), BF16)]
    grad_weight = call(halves_kernel, "halves", out, total, permute(total, other_core), joined, ins=order)[0]
    return grad_inputs, grad_q, grad_k, grad_weight


def solution(mesh):
    spread, sharded = P(("rep", "fsdp"), None), P("fsdp", None)
    line = P(("rep", "fsdp"))
    return jax.shard_map(
        body,
        mesh=mesh,
        in_specs=(spread, sharded, line, line, spread, spread, spread),
        out_specs=(spread, spread, spread, sharded),
        check_vma=False,
    )
```

```python
import jax
import jax.numpy as jnp
from jax import lax
from jax.experimental import pallas as pl
from jax.experimental.pallas import tpu as pltpu
from jax.sharding import PartitionSpec as P

KVH = 4
GROUP = 8
HD = 128
CAP = 8
TILE = 128
BLOCKS = TILE // CAP
AXES = ("rep", "fsdp")
F32 = jnp.float32
BF16 = jnp.bfloat16
NZL, NCO, NZH, NX, NY = 4, 2, 2, 4, 4
SLICES = NZH * NX
TOKEN = jax.ShapeDtypeStruct((8, 128), jnp.float32)
VMEM = pl.BlockSpec(memory_space=pltpu.VMEM)
ANY = pl.BlockSpec(memory_space=pl.ANY)


def permute(array, move):
    pairs = []
    for e in range(NZL * NCO * NZH * NX * NY):
        place = (e // 64, e // 32 % 2, e // 16 % 2, e // 4 % 4, e % 4)
        zl, co, zh, x, y = move(*place)
        pairs.append((e, (((zl * NCO + co) * NZH + zh) * NX + x % NX) * NY + y % NY))
    return lax.ppermute(array, AXES, pairs)


def along_y(k):
    return lambda zl, co, zh, x, y: (zl, co, zh, x, y + k)


def along_x(k):
    return lambda zl, co, zh, x, y: (zl, co, zh, x + k, y)


def other_core(zl, co, zh, x, y):
    return zl, 1 - co, zh, x, y


def mirror(zl, co, zh, x, y):
    return NZL - 1 - zl, co, 1 - zh, x, y


def flip_zl(bit):
    return lambda zl, co, zh, x, y: (zl ^ bit, co, zh, x, y)


def call(kernel, name, out, *args, ins=None, outs=None, scratch=(), mib=4, flops=0):
    size = sum(a.size * a.dtype.itemsize for a in args) + sum(o.size * o.dtype.itemsize for o in out)
    return pl.pallas_call(
        kernel,
        out_shape=out,
        in_specs=[VMEM] * len(args) if ins is None else ins,
        out_specs=[VMEM] * len(out) if outs is None else outs,
        scratch_shapes=scratch,
        compiler_params=pltpu.CompilerParams(vmem_limit_bytes=mib * 1024 * 1024),
        cost_estimate=pl.CostEstimate(flops=flops, bytes_accessed=size, transcendentals=0),
        name=name,
    )(*args)


def fetch(sources, targets, sems):
    copies = [pltpu.make_async_copy(s, t, sems.at[i]) for i, (s, t) in enumerate(zip(sources, targets, strict=True))]
    for copy in copies:
        copy.start()
    return copies


def at_place():
    rep, fsdp = lax.axis_index("rep"), lax.axis_index("fsdp")
    return lax.rem(rep, NCO), lax.div(fsdp, NX * NY), lax.rem(lax.div(fsdp, NY), NX), lax.rem(fsdp, NY)


def like(shape, dtype):
    return jax.ShapeDtypeStruct(shape, dtype)


def dot(a, b, over):
    return lax.dot_general(a, b, (((over[0],), (over[1],)), ((), ())), preferred_element_type=F32)


def feature_blocks(k):
    core, zh, x, y = at_place()
    for zr in range(NZH):
        for xr in range(NX):
            z = zh + zr - 2 * zh * zr
            slice_at = (z * NX + lax.rem(x - xr + NX, NX)) * NY + lax.rem(y + k, NY)
            for cr in range(NCO):
                yield (zr * NX + xr) * NCO + cr, slice_at * NCO + core + cr - 2 * core * cr


def finish(token):
    token[...] = jnp.zeros(token.shape, token.dtype)


def masks_kernel(slots_in, ids_in, masks, slots, ids, sems):
    copies = fetch((slots_in, ids_in), (slots, ids), sems)
    lane = lax.broadcasted_iota(jnp.int32, (CAP, TILE), 1) & (CAP - 1)
    sub = lax.broadcasted_iota(jnp.int32, (CAP, TILE), 0)
    causal = sub <= lane
    plain = causal.astype(jnp.int32)
    for p in range(masks.shape[0]):
        masks[p] = plain
    for copy in copies:
        copy.wait()
    for r in range(slots.shape[0] // CAP):
        keys = jnp.zeros((CAP, TILE), jnp.int32)
        rows = jnp.zeros((CAP, TILE), jnp.int32)
        for j in range(CAP):
            value = ids[r * CAP + j]
            keys = jnp.where(sub == j, value, keys)
            rows = jnp.where(lane == j, value, rows)
        masks[lax.div(slots[r * CAP], CAP)] = jnp.where((keys == rows) & causal, 1, 0)


def run_masks(slots, ids, peers):
    index = pltpu.SMEM(slots.shape, jnp.int32)
    scratch = (index, index, pltpu.SemaphoreType.DMA((2,)))
    out = [like((peers, CAP, TILE), jnp.int32)]
    return call(masks_kernel, "masks", out, slots, ids, ins=[ANY] * 2, scratch=scratch, mib=56)[0]


def split_kernel(full_in, after, p0, p1, p2, p3, full, sems):
    for copy in fetch((full_in,), (full,), sems):
        copy.wait()
    width = full.shape[1] // (NY * SLICES * NCO)
    for k, part in enumerate((p0, p1, p2, p3)):
        for at, block in feature_blocks(k):
            part[:, at * width : (at + 1) * width] = full[:, pl.ds(pl.multiple_of(block * width, width), width)]


def split(full, after):
    rows, columns = full.shape
    out = [like((rows, columns // NY), full.dtype)] * NY
    scratch = (pltpu.VMEM(full.shape, full.dtype), pltpu.SemaphoreType.DMA((1,)))
    return call(split_kernel, "split", out, full, after, ins=[ANY] * 2, scratch=scratch, mib=56)


def join_kernel(p0, p1, p2, p3, full):
    width = p0.shape[1] // (SLICES * NCO)
    for k, part in enumerate((p0, p1, p2, p3)):
        for at, block in feature_blocks(k):
            full[:, pl.ds(pl.multiple_of(block * width, width), width)] = part[:, at * width : (at + 1) * width]


def join(parts):
    rows, columns = parts[0].shape
    return call(join_kernel, "join", [like((rows, columns * NY), parts[0].dtype)], *parts, mib=56)[0]


def heads(block, t):
    rows = block[t * TILE : (t + 1) * TILE, :]
    return jnp.concatenate([rows[:, h * HD : (h + 1) * HD] for h in range(GROUP)], axis=0)


def own_block(lanes):
    return lax.broadcasted_iota(jnp.int32, (CAP, lanes), 1) % TILE // CAP


def fold(pairs, block):
    out = pairs[0:CAP]
    for b in range(1, BLOCKS):
        out = jnp.where(block == b, pairs[b * CAP : (b + 1) * CAP], out)
    return out


def unfold(folded, block):
    return jnp.concatenate([jnp.where(block == b, folded, 0.0) for b in range(BLOCKS)], axis=0).astype(BF16)


def head_blocks(array):
    width = GROUP * HD
    return [array.at[:, pl.ds(k * width, width)] for k in range(KVH)]


def scores_kernel(queries, keys_in, scores, q, keys, sems):
    copies = fetch([keys_in] + head_blocks(queries), [keys] + [q.at[k] for k in range(KVH)], sems)
    block = own_block(GROUP * TILE)
    copies[0].wait()
    for k in range(KVH):
        copies[1 + k].wait()
        for t in range(scores.shape[1]):
            pairs = dot(keys[t * TILE : (t + 1) * TILE, k * HD : (k + 1) * HD], heads(q[k], t), (1, 1))
            scores[k, t] = fold(pairs, block)


def probs_kernel(scores_in, masks_in, upstream, *rest):
    grad_v, probs, u, scores, masks, sems = rest[-6:]
    sources = [scores_in, masks_in] + head_blocks(upstream)
    copies = fetch(sources, [scores, masks] + [u.at[k] for k in range(KVH)], sems)
    small, block = own_block(TILE), own_block(GROUP * TILE)
    copies[0].wait()
    copies[1].wait()
    seen = []
    for t in range(scores.shape[1]):
        mask = masks[t * BLOCKS]
        for b in range(1, BLOCKS):
            mask = jnp.where(small == b, masks[t * BLOCKS + b], mask)
        seen.append(jnp.concatenate([mask] * GROUP, axis=1) != 0)
    for k in range(KVH):
        copies[2 + k].wait()
        for t, visible in enumerate(seen):
            masked = jnp.where(visible, scores[k, t] * (1.0 / HD**0.5), -1e30)
            top = jnp.max(masked, axis=0, keepdims=True)
            expo = jnp.where(visible, jnp.exp(masked - top), 0.0)
            prob = expo / jnp.sum(expo, axis=0, keepdims=True)
            probs[k, t] = prob
            grad = dot(unfold(prob, block), heads(u[k], t), (1, 0))
            grad_v[t * TILE : (t + 1) * TILE, k * HD : (k + 1) * HD] = grad.astype(BF16)


def dscore_kernel(probs, values, upstream, queries, keys, *rest):
    grad_q, grad_k = rest[-2:]
    scale = 1.0 / HD**0.5
    block = own_block(GROUP * TILE)
    for t in range(probs.shape[1]):
        rows = slice(t * TILE, (t + 1) * TILE)
        prob = probs[0, t]
        dprob = fold(dot(values[rows, :], heads(upstream, t), (1, 1)), block)
        delta = jnp.sum(prob * dprob, axis=0, keepdims=True)
        dscore = unfold(prob * (dprob - delta), block)
        grad_k[rows, :] = (dot(dscore, heads(queries, t), (1, 0)) * scale).astype(BF16)
        grad = (dot(dscore, keys[rows, :], (0, 0)) * scale).astype(BF16)
        for h in range(GROUP):
            grad_q[rows, h * HD : (h + 1) * HD] = grad[h * TILE : (h + 1) * TILE]


def per_head(kernel, name, ins, outs, args, flops):
    size = sum(a.size * a.dtype.itemsize for a in args) + sum(o.size * o.dtype.itemsize for o, _ in outs)
    return pl.pallas_call(
        kernel,
        grid=(KVH,),
        out_shape=[o for o, _ in outs],
        in_specs=ins,
        out_specs=[s for _, s in outs],
        compiler_params=pltpu.CompilerParams(vmem_limit_bytes=56 * 1024 * 1024),
        cost_estimate=pl.CostEstimate(flops=flops, bytes_accessed=size, transcendentals=0),
        name=name,
    )(*args)


def attention_specs(slots):
    wide = pl.BlockSpec((slots, GROUP * HD), lambda k: (0, k))
    narrow = pl.BlockSpec((slots, HD), lambda k: (0, k))
    tiles = slots // TILE
    folded = pl.BlockSpec((1, tiles, CAP, GROUP * TILE), lambda k: (k, 0, 0, 0))
    return wide, narrow, folded, like((KVH, tiles, CAP, GROUP * TILE), F32)


def folded_shape(slots):
    return (KVH, slots // TILE, CAP, GROUP * TILE)


def attention_scores(queries, keys):
    slots = queries.shape[0]
    sems = pltpu.SemaphoreType.DMA((1 + KVH,))
    scratch = (pltpu.VMEM((KVH, slots, GROUP * HD), BF16), pltpu.VMEM(keys.shape, BF16), sems)
    out = [like(folded_shape(slots), F32)]
    flops = 2 * queries.size * TILE
    return call(scores_kernel, "scores", out, queries, keys, ins=[ANY] * 2, scratch=scratch, mib=56, flops=flops)[0]


def attention_probs(scores, masks, upstream, after):
    slots = upstream.shape[0]
    u = pltpu.VMEM((KVH, slots, GROUP * HD), BF16)
    sems = pltpu.SemaphoreType.DMA((2 + KVH,))
    scratch = (u, pltpu.VMEM(scores.shape, F32), pltpu.VMEM(masks.shape, jnp.int32), sems)
    out = [like((slots, KVH * HD), BF16), like(scores.shape, F32)]
    flops = 2 * upstream.size * TILE
    ins = [ANY] * (3 + len(after))
    return call(probs_kernel, "probs", out, scores, masks, upstream, *after, ins=ins, scratch=scratch, mib=56, flops=flops)


def attention_dscore(probs, values, upstream, queries, keys, after):
    wide, narrow, folded, _ = attention_specs(queries.shape[0])
    outs = [(like(queries.shape, BF16), wide), (like(keys.shape, BF16), narrow)]
    args = (probs, values, upstream, queries, keys, *after)
    flops = 6 * upstream.size * TILE
    return per_head(dscore_kernel, "dscore", [folded, narrow, wide, wide, narrow] + [ANY] * len(after), outs, args, flops)


def slice_of(weights, s):
    half = weights.shape[1] // NZH
    rows = slice(s // NX * half, (s // NX + 1) * half)
    return jnp.concatenate([weights[cr * NX + s % NX, rows] for cr in range(NCO)], axis=0)


def partial_kernel(*refs):
    ins, (_, v0, v1, v2, v3, x, w, sems) = refs[: NY + SLICES], refs[NY + SLICES :]
    rows, width = x.shape[1], w.shape[1]
    copies = fetch(ins, [x.at[k] for k in range(NY)] + [w.at[i] for i in range(SLICES)], sems)
    for copy in copies:
        copy.wait()
    total = None
    for s in range(SLICES):
        stack = jnp.concatenate([x[k, :, s * width : (s + 1) * width] for k in range(NY)], axis=0)
        term = dot(stack, slice_of(w, s), (1, 0))
        total = term if total is None else total + term
    for k, out in enumerate((v0, v1, v2, v3)):
        out[...] = total[k * rows : (k + 1) * rows].astype(out.dtype)


def staged(*groups):
    stacks = [pltpu.VMEM((len(g), *g[0].shape), g[0].dtype) for g in groups]
    return (*stacks, pltpu.SemaphoreType.DMA((sum(map(len, groups)),)))


def partial_values(pieces, weights, after):
    rows, width = pieces[0].shape[0], weights[0].shape[1]
    out = [like((rows, width), F32)] + [like((rows, width), BF16)] * (NY - 1)
    flops = 2 * NY * pieces[0].size * width
    ins, scratch = [ANY] * (NY + SLICES + 1), staged(pieces, weights)
    return call(partial_kernel, "partial_values", out, *pieces, *weights, after, ins=ins, scratch=scratch, mib=56, flops=flops)


def place_kernel(slot, own, a, b, c, after, out):
    rows = own[...] + a[...].astype(F32) + b[...].astype(F32) + c[...].astype(F32)
    at = lax.broadcasted_iota(jnp.int32, (out.shape[0], own.shape[0]), 0)
    chosen = jnp.where(at == slot[...], 1.0, 0.0).astype(BF16)
    out[...] = dot(chosen, rows.astype(BF16), (1, 0)).astype(BF16)


def pick_kernel(*refs):
    slot, buffer, out = refs[0], refs[1], refs[-1]
    at = lax.broadcasted_iota(jnp.int32, (buffer.shape[0], out.shape[0]), 0)
    chosen = jnp.where(at == slot[...], 1.0, 0.0).astype(BF16)
    out[...] = dot(chosen, buffer[...], (0, 0)).astype(BF16)


def back_kernel(*refs):
    ins, (_, g0, g1, g2, g3, token, r, w, sems) = refs[: NY + SLICES], refs[NY + SLICES :]
    finish(token)
    rows, width = r.shape[1], w.shape[1]
    copies = fetch(ins, [r.at[k] for k in range(NY)] + [w.at[i] for i in range(SLICES)], sems)
    for copy in copies:
        copy.wait()
    stack = r[...].reshape(NY * rows, r.shape[2])
    for s in range(SLICES):
        grad = dot(stack, slice_of(w, s), (1, 1)).astype(BF16)
        for k, out in enumerate((g0, g1, g2, g3)):
            out[:, s * width : (s + 1) * width] = grad[k * rows : (k + 1) * rows]


def back(grads, weights, after):
    rows, width = grads[0].shape
    columns = SLICES * weights[0].shape[0]
    flops = 2 * NY * rows * width * columns
    ins, scratch = [ANY] * (NY + SLICES + 1), staged(grads, weights)
    out = [like((rows, columns), BF16)] * NY + [TOKEN]
    return call(back_kernel, "back", out, *grads, *weights, after, ins=ins, scratch=scratch, mib=56, flops=flops)


def share_kernel(*refs):
    ins, (own, other, token, x, r, sems) = refs[: 2 * NY], refs[-6:]
    finish(token)
    half = own.shape[1]
    copies = fetch(ins, [x.at[k] for k in range(NY)] + [r.at[k] for k in range(NY)], sems)
    for copy in copies:
        copy.wait()
    grads = r[...].reshape(NY * r.shape[1], r.shape[2])
    for s in range(SLICES):
        stack = jnp.concatenate([x[k, :, s * NCO * half : (s + 1) * NCO * half] for k in range(NY)], axis=0)
        share = dot(stack, grads, (0, 0))
        own[s] = share[:half]
        other[s] = share[half:].astype(other.dtype)


def shares(pieces, grads, after):
    half, width = pieces[0].shape[1] // SLICES // NCO, grads[0].shape[1]
    shape = (SLICES, half, width)
    flops = 2 * NY * pieces[0].size * width
    out = [like(shape, F32), like(shape, BF16), TOKEN]
    ins, scratch = [ANY] * (2 * NY + len(after)), staged(pieces, grads)
    return call(share_kernel, "shares", out, *pieces, *grads, *after, ins=ins, scratch=scratch, mib=20, flops=flops)


def core_sum_kernel(own, got, keep, s1, s2, s3):
    for zr in range(NZH):
        for xr, out in enumerate((keep, s1, s2, s3)):
            out[zr] = (own[zr * NX + xr] + got[zr * NX + xr].astype(F32)).astype(out.dtype)


def x_sum_kernel(keep, a, b, c, after, near, far):
    for zr, out in enumerate((near, far)):
        total = keep[zr] + a[zr].astype(F32) + b[zr].astype(F32) + c[zr].astype(F32)
        out[...] = total.astype(out.dtype)


def stack_kernel(a, b, out):
    rows = a.shape[0] // NCO
    here = pl.ds(pl.multiple_of(at_place()[0] * rows, rows), rows)
    out[:rows] = a[here, :]
    out[rows:] = b[here, :]


def pair_sum_kernel(*refs):
    a, b, out = refs[0], refs[1], refs[-1]
    out[...] = (a[...].astype(F32) + b[...].astype(F32)).astype(out.dtype)


def halves_kernel(mine, other, out):
    core, rows = at_place()[0], mine.shape[0]
    out[pl.ds(pl.multiple_of(core * rows, rows), rows), :] = mine[...]
    out[pl.ds(pl.multiple_of((1 - core) * rows, rows), rows), :] = other[...]


def body(inputs, value_weight, send_slot, response_id, queries, keys, upstream):
    peers = lax.axis_size("fsdp")
    slots, rows = queries.shape[0], inputs.shape[0]
    half, width = value_weight.shape[0] // NCO, value_weight.shape[1]
    slot = send_slot.reshape(1, rows)

    def exchange(buffer):
        return lax.all_to_all(buffer, "fsdp", split_axis=0, concat_axis=0, tiled=True)

    mask = run_masks(send_slot, response_id, peers)
    masks = exchange(mask)
    mirrored = permute(value_weight, mirror)
    pieces = split(inputs, mask)
    pieces = [pieces[0]] + [permute(pieces[k], along_y(k)) for k in range(1, NY)]
    pair = call(stack_kernel, "pair", [like((NZH * half, width), BF16)], value_weight, mirrored)[0]
    weights = [pair] + [permute(pair, along_x(k)) for k in range(1, NX)]
    weights += [permute(weight, other_core) for weight in weights]

    scores = attention_scores(queries, keys)
    grad_v, probs = attention_probs(scores, masks, upstream, (pair,))
    returned = exchange(grad_v)
    order, out = [VMEM] * 2 + [ANY] * (NY - 1), [like((rows, width), BF16)]
    row_grad = call(pick_kernel, "pick", out, slot, returned, *pieces[1:], ins=order)[0]
    grads = [row_grad] + [permute(row_grad, along_y(k)) for k in range(1, NY)]

    own, other, shared = shares(pieces, grads, weights[1:NX])
    partial, *parts = partial_values(pieces, weights, shared)
    parts = [permute(part, along_y(-k)) for k, part in enumerate(parts, 1)]
    got = permute(other, other_core)
    out = [like((NZH, half, width), F32)] + [like((NZH, half, width), BF16)] * (NX - 1)
    keep, *sends = call(core_sum_kernel, "core_sum", out, own, got, mib=8)
    arrived = [permute(send, along_x(-k)) for k, send in enumerate(sends, 1)]

    mine, *sends, backed = back(grads, weights, keep)
    columns = [mine] + [permute(send, along_y(-k)) for k, send in enumerate(sends, 1)]

    out = [like((half, width), F32), like((half, width), BF16)]
    near, far = call(x_sum_kernel, "x_sum", out, keep, *arrived, backed, ins=[VMEM] * NX + [ANY])
    small = [like((half, width), BF16)]
    total = call(pair_sum_kernel, "mirror_sum", small, near, permute(far, mirror), *parts, ins=[VMEM] * 2 + [ANY] * (NY - 1))[0]

    after, out = [VMEM] * 5 + [ANY], [like((slots, width), BF16)]
    value_buffer = call(place_kernel, "place", out, slot, partial, *parts, total, ins=after)[0]
    values = exchange(value_buffer)
    grad_q, grad_k = attention_dscore(probs, values, upstream, queries, keys, columns[1:])
    grad_inputs = join(columns)

    for bit in (1, 2):
        total = call(pair_sum_kernel, "z_sum", small, total, permute(total, flip_zl(bit)))[0]
    out = [like((NCO * half, width), BF16)]
    grad_weight = call(halves_kernel, "halves", out, total, permute(total, other_core))[0]
    return grad_inputs, grad_q, grad_k, grad_weight


def solution(mesh):
    spread, sharded = P(("rep", "fsdp"), None), P("fsdp", None)
    line = P(("rep", "fsdp"))
    return jax.shard_map(
        body,
        mesh=mesh,
        in_specs=(spread, sharded, line, line, spread, spread, spread),
        out_specs=(spread, spread, spread, sharded),
        check_vma=False,
    )
```

```python
import jax
import jax.numpy as jnp
from jax import lax
from jax.experimental import pallas as pl
from jax.experimental.pallas import tpu as pltpu
from jax.sharding import PartitionSpec as P

KVH = 4
GROUP = 8
HD = 128
CAP = 8
TILE = 128
BLOCKS = TILE // CAP
AXES = ("rep", "fsdp")
F32 = jnp.float32
BF16 = jnp.bfloat16
NZL, NCO, NZH, NX, NY = 4, 2, 2, 4, 4
SLICES = NZH * NX
TOKEN = jax.ShapeDtypeStruct((8, 128), jnp.float32)
VMEM = pl.BlockSpec(memory_space=pltpu.VMEM)
ANY = pl.BlockSpec(memory_space=pl.ANY)


def permute(array, move):
    pairs = []
    for e in range(NZL * NCO * NZH * NX * NY):
        place = (e // 64, e // 32 % 2, e // 16 % 2, e // 4 % 4, e % 4)
        zl, co, zh, x, y = move(*place)
        pairs.append((e, (((zl * NCO + co) * NZH + zh) * NX + x % NX) * NY + y % NY))
    return lax.ppermute(array, AXES, pairs)


def along_y(k):
    return lambda zl, co, zh, x, y: (zl, co, zh, x, y + k)


def along_x(k):
    return lambda zl, co, zh, x, y: (zl, co, zh, x + k, y)


def other_core(zl, co, zh, x, y):
    return zl, 1 - co, zh, x, y


def mirror(zl, co, zh, x, y):
    return NZL - 1 - zl, co, 1 - zh, x, y


def flip_zl(bit):
    return lambda zl, co, zh, x, y: (zl ^ bit, co, zh, x, y)


def call(kernel, name, out, *args, ins=None, outs=None, scratch=(), mib=4, flops=0):
    size = sum(a.size * a.dtype.itemsize for a in args) + sum(o.size * o.dtype.itemsize for o in out)
    return pl.pallas_call(
        kernel,
        out_shape=out,
        in_specs=[VMEM] * len(args) if ins is None else ins,
        out_specs=[VMEM] * len(out) if outs is None else outs,
        scratch_shapes=scratch,
        compiler_params=pltpu.CompilerParams(vmem_limit_bytes=mib * 1024 * 1024),
        cost_estimate=pl.CostEstimate(flops=flops, bytes_accessed=size, transcendentals=0),
        name=name,
    )(*args)


def fetch(sources, targets, sems):
    copies = [pltpu.make_async_copy(s, t, sems.at[i]) for i, (s, t) in enumerate(zip(sources, targets, strict=True))]
    for copy in copies:
        copy.start()
    return copies


def at_place():
    rep, fsdp = lax.axis_index("rep"), lax.axis_index("fsdp")
    return lax.rem(rep, NCO), lax.div(fsdp, NX * NY), lax.rem(lax.div(fsdp, NY), NX), lax.rem(fsdp, NY)


def like(shape, dtype):
    return jax.ShapeDtypeStruct(shape, dtype)


def dot(a, b, over):
    return lax.dot_general(a, b, (((over[0],), (over[1],)), ((), ())), preferred_element_type=F32)


def feature_blocks(k):
    core, zh, x, y = at_place()
    for zr in range(NZH):
        for xr in range(NX):
            z = zh + zr - 2 * zh * zr
            slice_at = (z * NX + lax.rem(x - xr + NX, NX)) * NY + lax.rem(y + k, NY)
            for cr in range(NCO):
                yield (zr * NX + xr) * NCO + cr, slice_at * NCO + core + cr - 2 * core * cr


def finish(token):
    token[...] = jnp.zeros(token.shape, token.dtype)


def masks_kernel(slots_in, ids_in, masks, slots, ids, sems):
    copies = fetch((slots_in, ids_in), (slots, ids), sems)
    lane = lax.broadcasted_iota(jnp.int32, (CAP, TILE), 1) & (CAP - 1)
    sub = lax.broadcasted_iota(jnp.int32, (CAP, TILE), 0)
    causal = sub <= lane
    plain = causal.astype(jnp.int32)
    for p in range(masks.shape[0]):
        masks[p] = plain
    for copy in copies:
        copy.wait()
    for r in range(slots.shape[0] // CAP):
        keys = jnp.zeros((CAP, TILE), jnp.int32)
        rows = jnp.zeros((CAP, TILE), jnp.int32)
        for j in range(CAP):
            value = ids[r * CAP + j]
            keys = jnp.where(sub == j, value, keys)
            rows = jnp.where(lane == j, value, rows)
        masks[lax.div(slots[r * CAP], CAP)] = jnp.where((keys == rows) & causal, 1, 0)


def run_masks(slots, ids, peers):
    index = pltpu.SMEM(slots.shape, jnp.int32)
    scratch = (index, index, pltpu.SemaphoreType.DMA((2,)))
    out = [like((peers, CAP, TILE), jnp.int32)]
    return call(masks_kernel, "masks", out, slots, ids, ins=[ANY] * 2, scratch=scratch, mib=56)[0]


def split_kernel(full_in, after, p0, p1, p2, p3, full, sems):
    for copy in fetch((full_in,), (full,), sems):
        copy.wait()
    width = full.shape[1] // (NY * SLICES * NCO)
    for k, part in enumerate((p0, p1, p2, p3)):
        for at, block in feature_blocks(k):
            part[:, at * width : (at + 1) * width] = full[:, pl.ds(pl.multiple_of(block * width, width), width)]


def split(full, after):
    rows, columns = full.shape
    out = [like((rows, columns // NY), full.dtype)] * NY
    scratch = (pltpu.VMEM(full.shape, full.dtype), pltpu.SemaphoreType.DMA((1,)))
    return call(split_kernel, "split", out, full, after, ins=[ANY] * 2, scratch=scratch, mib=48)


def join_kernel(p0, p1, p2, p3, full):
    width = p0.shape[1] // (SLICES * NCO)
    for k, part in enumerate((p0, p1, p2, p3)):
        for at, block in feature_blocks(k):
            full[:, pl.ds(pl.multiple_of(block * width, width), width)] = part[:, at * width : (at + 1) * width]


def join(parts):
    rows, columns = parts[0].shape
    return call(join_kernel, "join", [like((rows, columns * NY), parts[0].dtype)], *parts, mib=48)[0]


def heads(block, t):
    rows = block[t * TILE : (t + 1) * TILE, :]
    return jnp.concatenate([rows[:, h * HD : (h + 1) * HD] for h in range(GROUP)], axis=0)


def own_block(lanes):
    return lax.broadcasted_iota(jnp.int32, (CAP, lanes), 1) % TILE // CAP


def fold(pairs, block):
    out = pairs[0:CAP]
    for b in range(1, BLOCKS):
        out = jnp.where(block == b, pairs[b * CAP : (b + 1) * CAP], out)
    return out


def unfold(folded, block):
    return jnp.concatenate([jnp.where(block == b, folded, 0.0) for b in range(BLOCKS)], axis=0).astype(BF16)


def head_blocks(array):
    width = GROUP * HD
    return [array.at[:, pl.ds(k * width, width)] for k in range(KVH)]


def scores_kernel(queries, keys_in, scores, q, keys, sems):
    copies = fetch([keys_in] + head_blocks(queries), [keys] + [q.at[k] for k in range(KVH)], sems)
    block = own_block(GROUP * TILE)
    copies[0].wait()
    for k in range(KVH):
        copies[1 + k].wait()
        for t in range(scores.shape[1]):
            pairs = dot(keys[t * TILE : (t + 1) * TILE, k * HD : (k + 1) * HD], heads(q[k], t), (1, 1))
            scores[k, t] = fold(pairs, block)


def probs_kernel(scores_in, masks_in, upstream, *rest):
    grad_v, probs, u, scores, masks, sems = rest[-6:]
    sources = [scores_in, masks_in] + head_blocks(upstream)
    copies = fetch(sources, [scores, masks] + [u.at[k] for k in range(KVH)], sems)
    small, block = own_block(TILE), own_block(GROUP * TILE)
    copies[0].wait()
    copies[1].wait()
    seen = []
    for t in range(scores.shape[1]):
        mask = masks[t * BLOCKS]
        for b in range(1, BLOCKS):
            mask = jnp.where(small == b, masks[t * BLOCKS + b], mask)
        seen.append(jnp.concatenate([mask] * GROUP, axis=1) != 0)
    for k in range(KVH):
        copies[2 + k].wait()
        for t, visible in enumerate(seen):
            masked = jnp.where(visible, scores[k, t] * (1.0 / HD**0.5), -1e30)
            top = jnp.max(masked, axis=0, keepdims=True)
            expo = jnp.where(visible, jnp.exp(masked - top), 0.0)
            prob = expo / jnp.sum(expo, axis=0, keepdims=True)
            probs[k, t] = prob
            grad = dot(unfold(prob, block), heads(u[k], t), (1, 0))
            grad_v[t * TILE : (t + 1) * TILE, k * HD : (k + 1) * HD] = grad.astype(BF16)


def dscore_kernel(probs, values, upstream, queries, keys, *rest):
    grad_q, grad_k = rest[-2:]
    scale = 1.0 / HD**0.5
    block = own_block(GROUP * TILE)
    for t in range(probs.shape[1]):
        rows = slice(t * TILE, (t + 1) * TILE)
        prob = probs[0, t]
        dprob = fold(dot(values[rows, :], heads(upstream, t), (1, 1)), block)
        delta = jnp.sum(prob * dprob, axis=0, keepdims=True)
        dscore = unfold(prob * (dprob - delta), block)
        grad_k[rows, :] = (dot(dscore, heads(queries, t), (1, 0)) * scale).astype(BF16)
        grad = (dot(dscore, keys[rows, :], (0, 0)) * scale).astype(BF16)
        for h in range(GROUP):
            grad_q[rows, h * HD : (h + 1) * HD] = grad[h * TILE : (h + 1) * TILE]


def per_head(kernel, name, ins, outs, args, flops):
    size = sum(a.size * a.dtype.itemsize for a in args) + sum(o.size * o.dtype.itemsize for o, _ in outs)
    return pl.pallas_call(
        kernel,
        grid=(KVH,),
        out_shape=[o for o, _ in outs],
        in_specs=ins,
        out_specs=[s for _, s in outs],
        compiler_params=pltpu.CompilerParams(vmem_limit_bytes=48 * 1024 * 1024),
        cost_estimate=pl.CostEstimate(flops=flops, bytes_accessed=size, transcendentals=0),
        name=name,
    )(*args)


def attention_specs(slots):
    wide = pl.BlockSpec((slots, GROUP * HD), lambda k: (0, k))
    narrow = pl.BlockSpec((slots, HD), lambda k: (0, k))
    tiles = slots // TILE
    folded = pl.BlockSpec((1, tiles, CAP, GROUP * TILE), lambda k: (k, 0, 0, 0))
    return wide, narrow, folded, like((KVH, tiles, CAP, GROUP * TILE), F32)


def folded_shape(slots):
    return (KVH, slots // TILE, CAP, GROUP * TILE)


def attention_scores(queries, keys):
    slots = queries.shape[0]
    sems = pltpu.SemaphoreType.DMA((1 + KVH,))
    scratch = (pltpu.VMEM((KVH, slots, GROUP * HD), BF16), pltpu.VMEM(keys.shape, BF16), sems)
    out = [like(folded_shape(slots), F32)]
    flops = 2 * queries.size * TILE
    return call(scores_kernel, "scores", out, queries, keys, ins=[ANY] * 2, scratch=scratch, mib=48, flops=flops)[0]


def attention_probs(scores, masks, upstream, after):
    slots = upstream.shape[0]
    u = pltpu.VMEM((KVH, slots, GROUP * HD), BF16)
    sems = pltpu.SemaphoreType.DMA((2 + KVH,))
    scratch = (u, pltpu.VMEM(scores.shape, F32), pltpu.VMEM(masks.shape, jnp.int32), sems)
    out = [like((slots, KVH * HD), BF16), like(scores.shape, F32)]
    flops = 2 * upstream.size * TILE
    ins = [ANY] * (3 + len(after))
    return call(probs_kernel, "probs", out, scores, masks, upstream, *after, ins=ins, scratch=scratch, mib=48, flops=flops)


def attention_dscore(probs, values, upstream, queries, keys, after):
    wide, narrow, folded, _ = attention_specs(queries.shape[0])
    outs = [(like(queries.shape, BF16), wide), (like(keys.shape, BF16), narrow)]
    args = (probs, values, upstream, queries, keys, *after)
    flops = 6 * upstream.size * TILE
    return per_head(dscore_kernel, "dscore", [folded, narrow, wide, wide, narrow] + [ANY] * len(after), outs, args, flops)


def slice_of(weights, s):
    half = weights.shape[1] // NZH
    rows = slice(s // NX * half, (s // NX + 1) * half)
    return jnp.concatenate([weights[cr * NX + s % NX, rows] for cr in range(NCO)], axis=0)


def partial_kernel(*refs):
    ins, (_, v0, v1, v2, v3, x, w, sems) = refs[: NY + SLICES], refs[NY + SLICES :]
    rows, width = x.shape[1], w.shape[1]
    copies = fetch(ins, [x.at[k] for k in range(NY)] + [w.at[i] for i in range(SLICES)], sems)
    for copy in copies:
        copy.wait()
    total = None
    for s in range(SLICES):
        stack = jnp.concatenate([x[k, :, s * width : (s + 1) * width] for k in range(NY)], axis=0)
        term = dot(stack, slice_of(w, s), (1, 0))
        total = term if total is None else total + term
    for k, out in enumerate((v0, v1, v2, v3)):
        out[...] = total[k * rows : (k + 1) * rows].astype(out.dtype)


def staged(*groups):
    stacks = [pltpu.VMEM((len(g), *g[0].shape), g[0].dtype) for g in groups]
    return (*stacks, pltpu.SemaphoreType.DMA((sum(map(len, groups)),)))


def partial_values(pieces, weights, after):
    rows, width = pieces[0].shape[0], weights[0].shape[1]
    out = [like((rows, width), F32)] + [like((rows, width), BF16)] * (NY - 1)
    flops = 2 * NY * pieces[0].size * width
    ins, scratch = [ANY] * (NY + SLICES + 1), staged(pieces, weights)
    return call(partial_kernel, "partial_values", out, *pieces, *weights, after, ins=ins, scratch=scratch, mib=48, flops=flops)


def place_kernel(slot, own, a, b, c, after, out):
    rows = own[...] + a[...].astype(F32) + b[...].astype(F32) + c[...].astype(F32)
    at = lax.broadcasted_iota(jnp.int32, (out.shape[0], own.shape[0]), 0)
    chosen = jnp.where(at == slot[...], 1.0, 0.0).astype(BF16)
    out[...] = dot(chosen, rows.astype(BF16), (1, 0)).astype(BF16)


def pick_kernel(*refs):
    slot, buffer, out = refs[0], refs[1], refs[-1]
    at = lax.broadcasted_iota(jnp.int32, (buffer.shape[0], out.shape[0]), 0)
    chosen = jnp.where(at == slot[...], 1.0, 0.0).astype(BF16)
    out[...] = dot(chosen, buffer[...], (0, 0)).astype(BF16)


def back_kernel(*refs):
    ins, (_, g0, g1, g2, g3, token, r, w, sems) = refs[: NY + SLICES], refs[NY + SLICES :]
    finish(token)
    rows, width = r.shape[1], w.shape[1]
    copies = fetch(ins, [r.at[k] for k in range(NY)] + [w.at[i] for i in range(SLICES)], sems)
    for copy in copies:
        copy.wait()
    stack = r[...].reshape(NY * rows, r.shape[2])
    for s in range(SLICES):
        grad = dot(stack, slice_of(w, s), (1, 1)).astype(BF16)
        for k, out in enumerate((g0, g1, g2, g3)):
            out[:, s * width : (s + 1) * width] = grad[k * rows : (k + 1) * rows]


def back(grads, weights, after):
    rows, width = grads[0].shape
    columns = SLICES * weights[0].shape[0]
    flops = 2 * NY * rows * width * columns
    ins, scratch = [ANY] * (NY + SLICES + 1), staged(grads, weights)
    out = [like((rows, columns), BF16)] * NY + [TOKEN]
    return call(back_kernel, "back", out, *grads, *weights, after, ins=ins, scratch=scratch, mib=48, flops=flops)


def share_kernel(*refs):
    ins, (own, other, token, x, r, sems) = refs[: 2 * NY], refs[-6:]
    finish(token)
    half = own.shape[1]
    copies = fetch(ins, [x.at[k] for k in range(NY)] + [r.at[k] for k in range(NY)], sems)
    for copy in copies:
        copy.wait()
    grads = r[...].reshape(NY * r.shape[1], r.shape[2])
    for s in range(SLICES):
        stack = jnp.concatenate([x[k, :, s * NCO * half : (s + 1) * NCO * half] for k in range(NY)], axis=0)
        share = dot(stack, grads, (0, 0))
        own[s] = share[:half]
        other[s] = share[half:].astype(other.dtype)


def shares(pieces, grads, after):
    half, width = pieces[0].shape[1] // SLICES // NCO, grads[0].shape[1]
    shape = (SLICES, half, width)
    flops = 2 * NY * pieces[0].size * width
    out = [like(shape, F32), like(shape, BF16), TOKEN]
    ins, scratch = [ANY] * (2 * NY + len(after)), staged(pieces, grads)
    return call(share_kernel, "shares", out, *pieces, *grads, *after, ins=ins, scratch=scratch, mib=20, flops=flops)


def core_sum_kernel(own, got, keep, s1, s2, s3):
    for zr in range(NZH):
        for xr, out in enumerate((keep, s1, s2, s3)):
            out[zr] = (own[zr * NX + xr] + got[zr * NX + xr].astype(F32)).astype(out.dtype)


def x_sum_kernel(keep, a, b, c, after, near, far):
    for zr, out in enumerate((near, far)):
        total = keep[zr] + a[zr].astype(F32) + b[zr].astype(F32) + c[zr].astype(F32)
        out[...] = total.astype(out.dtype)


def stack_kernel(a, b, out):
    rows = a.shape[0] // NCO
    here = pl.ds(pl.multiple_of(at_place()[0] * rows, rows), rows)
    out[:rows] = a[here, :]
    out[rows:] = b[here, :]


def pair_sum_kernel(*refs):
    a, b, out = refs[0], refs[1], refs[-1]
    out[...] = (a[...].astype(F32) + b[...].astype(F32)).astype(out.dtype)


def halves_kernel(mine, other, out):
    core, rows = at_place()[0], mine.shape[0]
    out[pl.ds(pl.multiple_of(core * rows, rows), rows), :] = mine[...]
    out[pl.ds(pl.multiple_of((1 - core) * rows, rows), rows), :] = other[...]


def body(inputs, value_weight, send_slot, response_id, queries, keys, upstream):
    peers = lax.axis_size("fsdp")
    slots, rows = queries.shape[0], inputs.shape[0]
    half, width = value_weight.shape[0] // NCO, value_weight.shape[1]
    slot = send_slot.reshape(1, rows)

    def exchange(buffer):
        return lax.all_to_all(buffer, "fsdp", split_axis=0, concat_axis=0, tiled=True)

    mask = run_masks(send_slot, response_id, peers)
    masks = exchange(mask)
    mirrored = permute(value_weight, mirror)
    pieces = split(inputs, mask)
    pieces = [pieces[0]] + [permute(pieces[k], along_y(k)) for k in range(1, NY)]
    pair = call(stack_kernel, "pair", [like((NZH * half, width), BF16)], value_weight, mirrored)[0]
    weights = [pair] + [permute(pair, along_x(k)) for k in range(1, NX)]
    weights += [permute(weight, other_core) for weight in weights]

    scores = attention_scores(queries, keys)
    grad_v, probs = attention_probs(scores, masks, upstream, (pair,))
    returned = exchange(grad_v)
    order, out = [VMEM] * 2 + [ANY] * (NY - 1), [like((rows, width), BF16)]
    row_grad = call(pick_kernel, "pick", out, slot, returned, *pieces[1:], ins=order)[0]
    grads = [row_grad] + [permute(row_grad, along_y(k)) for k in range(1, NY)]

    own, other, shared = shares(pieces, grads, weights[1:NX])
    partial, *parts = partial_values(pieces, weights, shared)
    parts = [permute(part, along_y(-k)) for k, part in enumerate(parts, 1)]
    got = permute(other, other_core)
    out = [like((NZH, half, width), F32)] + [like((NZH, half, width), BF16)] * (NX - 1)
    keep, *sends = call(core_sum_kernel, "core_sum", out, own, got, mib=8)
    arrived = [permute(send, along_x(-k)) for k, send in enumerate(sends, 1)]

    mine, *sends, backed = back(grads, weights, keep)
    columns = [mine] + [permute(send, along_y(-k)) for k, send in enumerate(sends, 1)]

    out = [like((half, width), F32), like((half, width), BF16)]
    near, far = call(x_sum_kernel, "x_sum", out, keep, *arrived, backed, ins=[VMEM] * NX + [ANY])
    small = [like((half, width), BF16)]
    total = call(pair_sum_kernel, "mirror_sum", small, near, permute(far, mirror), *parts, ins=[VMEM] * 2 + [ANY] * (NY - 1))[0]

    after, out = [VMEM] * 5 + [ANY], [like((slots, width), BF16)]
    value_buffer = call(place_kernel, "place", out, slot, partial, *parts, total, ins=after)[0]
    values = exchange(value_buffer)
    grad_q, grad_k = attention_dscore(probs, values, upstream, queries, keys, columns[1:])
    grad_inputs = join(columns)

    for bit in (1, 2):
        total = call(pair_sum_kernel, "z_sum", small, total, permute(total, flip_zl(bit)))[0]
    out = [like((NCO * half, width), BF16)]
    grad_weight = call(halves_kernel, "halves", out, total, permute(total, other_core))[0]
    return grad_inputs, grad_q, grad_k, grad_weight


def solution(mesh):
    spread, sharded = P(("rep", "fsdp"), None), P("fsdp", None)
    line = P(("rep", "fsdp"))
    return jax.shard_map(
        body,
        mesh=mesh,
        in_specs=(spread, sharded, line, line, spread, spread, spread),
        out_specs=(spread, spread, spread, sharded),
        check_vma=False,
    )
```

```python
import jax
import jax.numpy as jnp
from jax import lax
from jax.experimental import pallas as pl
from jax.experimental.pallas import tpu as pltpu
from jax.sharding import PartitionSpec as P

KVH = 4
GROUP = 8
HD = 128
CAP = 8
TILE = 128
BLOCKS = TILE // CAP
AXES = ("rep", "fsdp")
F32 = jnp.float32
BF16 = jnp.bfloat16
NZL, NCO, NZH, NX, NY = 4, 2, 2, 4, 4
SLICES = NZH * NX
TOKEN = jax.ShapeDtypeStruct((8, 128), jnp.float32)
VMEM = pl.BlockSpec(memory_space=pltpu.VMEM)
ANY = pl.BlockSpec(memory_space=pl.ANY)


def permute(array, move):
    pairs = []
    for e in range(NZL * NCO * NZH * NX * NY):
        place = (e // 64, e // 32 % 2, e // 16 % 2, e // 4 % 4, e % 4)
        zl, co, zh, x, y = move(*place)
        pairs.append((e, (((zl * NCO + co) * NZH + zh) * NX + x % NX) * NY + y % NY))
    return lax.ppermute(array, AXES, pairs)


def along_y(k):
    return lambda zl, co, zh, x, y: (zl, co, zh, x, y + k)


def along_x(k):
    return lambda zl, co, zh, x, y: (zl, co, zh, x + k, y)


def other_core(zl, co, zh, x, y):
    return zl, 1 - co, zh, x, y


def mirror(zl, co, zh, x, y):
    return NZL - 1 - zl, co, 1 - zh, x, y


def flip_zl(bit):
    return lambda zl, co, zh, x, y: (zl ^ bit, co, zh, x, y)


def call(kernel, name, out, *args, ins=None, outs=None, scratch=(), mib=4, flops=0):
    size = sum(a.size * a.dtype.itemsize for a in args) + sum(o.size * o.dtype.itemsize for o in out)
    return pl.pallas_call(
        kernel,
        out_shape=out,
        in_specs=[VMEM] * len(args) if ins is None else ins,
        out_specs=[VMEM] * len(out) if outs is None else outs,
        scratch_shapes=scratch,
        compiler_params=pltpu.CompilerParams(vmem_limit_bytes=mib * 1024 * 1024),
        cost_estimate=pl.CostEstimate(flops=flops, bytes_accessed=size, transcendentals=0),
        name=name,
    )(*args)


def fetch(sources, targets, sems):
    copies = [pltpu.make_async_copy(s, t, sems.at[i]) for i, (s, t) in enumerate(zip(sources, targets, strict=True))]
    for copy in copies:
        copy.start()
    return copies


def at_place():
    rep, fsdp = lax.axis_index("rep"), lax.axis_index("fsdp")
    return lax.rem(rep, NCO), lax.div(fsdp, NX * NY), lax.rem(lax.div(fsdp, NY), NX), lax.rem(fsdp, NY)


def like(shape, dtype):
    return jax.ShapeDtypeStruct(shape, dtype)


def dot(a, b, over):
    return lax.dot_general(a, b, (((over[0],), (over[1],)), ((), ())), preferred_element_type=F32)


def feature_blocks(k):
    core, zh, x, y = at_place()
    for zr in range(NZH):
        for xr in range(NX):
            z = zh + zr - 2 * zh * zr
            slice_at = (z * NX + lax.rem(x - xr + NX, NX)) * NY + lax.rem(y + k, NY)
            for cr in range(NCO):
                yield (zr * NX + xr) * NCO + cr, slice_at * NCO + core + cr - 2 * core * cr


def finish(token):
    token[...] = jnp.zeros(token.shape, token.dtype)


def masks_kernel(slots_in, ids_in, masks, slots, ids, sems):
    copies = fetch((slots_in, ids_in), (slots, ids), sems)
    lane = lax.broadcasted_iota(jnp.int32, (CAP, TILE), 1) & (CAP - 1)
    sub = lax.broadcasted_iota(jnp.int32, (CAP, TILE), 0)
    causal = sub <= lane
    plain = causal.astype(jnp.int32)
    for p in range(masks.shape[0]):
        masks[p] = plain
    for copy in copies:
        copy.wait()
    for r in range(slots.shape[0] // CAP):
        keys = jnp.zeros((CAP, TILE), jnp.int32)
        rows = jnp.zeros((CAP, TILE), jnp.int32)
        for j in range(CAP):
            value = ids[r * CAP + j]
            keys = jnp.where(sub == j, value, keys)
            rows = jnp.where(lane == j, value, rows)
        masks[lax.div(slots[r * CAP], CAP)] = jnp.where((keys == rows) & causal, 1, 0)


def run_masks(slots, ids, peers):
    index = pltpu.SMEM(slots.shape, jnp.int32)
    scratch = (index, index, pltpu.SemaphoreType.DMA((2,)))
    out = [like((peers, CAP, TILE), jnp.int32)]
    return call(masks_kernel, "masks", out, slots, ids, ins=[ANY] * 2, scratch=scratch, mib=56)[0]


def split_kernel(full_in, after, p0, p1, p2, p3, full, sems):
    for copy in fetch((full_in,), (full,), sems):
        copy.wait()
    width = full.shape[1] // (NY * SLICES * NCO)
    for k, part in enumerate((p0, p1, p2, p3)):
        for at, block in feature_blocks(k):
            part[:, at * width : (at + 1) * width] = full[:, pl.ds(pl.multiple_of(block * width, width), width)]


def split(full, after):
    rows, columns = full.shape
    out = [like((rows, columns // NY), full.dtype)] * NY
    scratch = (pltpu.VMEM(full.shape, full.dtype), pltpu.SemaphoreType.DMA((1,)))
    return call(split_kernel, "split", out, full, after, ins=[ANY] * 2, scratch=scratch, mib=56)


def join_kernel(p0, p1, p2, p3, full, token):
    finish(token)
    width = p0.shape[1] // (SLICES * NCO)
    for k, part in enumerate((p0, p1, p2, p3)):
        for at, block in feature_blocks(k):
            full[:, pl.ds(pl.multiple_of(block * width, width), width)] = part[:, at * width : (at + 1) * width]


def join(parts):
    rows, columns = parts[0].shape
    return call(join_kernel, "join", [like((rows, columns * NY), parts[0].dtype), TOKEN], *parts, mib=56)


def heads(block, t):
    rows = block[t * TILE : (t + 1) * TILE, :]
    return jnp.concatenate([rows[:, h * HD : (h + 1) * HD] for h in range(GROUP)], axis=0)


def own_block(lanes):
    return lax.broadcasted_iota(jnp.int32, (CAP, lanes), 1) % TILE // CAP


def fold(pairs, block):
    out = pairs[0:CAP]
    for b in range(1, BLOCKS):
        out = jnp.where(block == b, pairs[b * CAP : (b + 1) * CAP], out)
    return out


def unfold(folded, block):
    return jnp.concatenate([jnp.where(block == b, folded, 0.0) for b in range(BLOCKS)], axis=0).astype(BF16)


def head_blocks(array):
    width = GROUP * HD
    return [array.at[:, pl.ds(k * width, width)] for k in range(KVH)]


def scores_kernel(queries, keys_in, scores, q, keys, sems):
    copies = fetch([keys_in] + head_blocks(queries), [keys] + [q.at[k] for k in range(KVH)], sems)
    block = own_block(GROUP * TILE)
    copies[0].wait()
    for k in range(KVH):
        copies[1 + k].wait()
        for t in range(scores.shape[1]):
            pairs = dot(keys[t * TILE : (t + 1) * TILE, k * HD : (k + 1) * HD], heads(q[k], t), (1, 1))
            scores[k, t] = fold(pairs, block)


def probs_kernel(scores_in, masks_in, upstream, *rest):
    grad_v, probs, u, scores, masks, sems = rest[-6:]
    sources = [scores_in, masks_in] + head_blocks(upstream)
    copies = fetch(sources, [scores, masks] + [u.at[k] for k in range(KVH)], sems)
    small, block = own_block(TILE), own_block(GROUP * TILE)
    copies[0].wait()
    copies[1].wait()
    seen = []
    for t in range(scores.shape[1]):
        mask = masks[t * BLOCKS]
        for b in range(1, BLOCKS):
            mask = jnp.where(small == b, masks[t * BLOCKS + b], mask)
        seen.append(jnp.concatenate([mask] * GROUP, axis=1) != 0)
    for k in range(KVH):
        copies[2 + k].wait()
        for t, visible in enumerate(seen):
            masked = jnp.where(visible, scores[k, t] * (1.0 / HD**0.5), -1e30)
            top = jnp.max(masked, axis=0, keepdims=True)
            expo = jnp.where(visible, jnp.exp(masked - top), 0.0)
            prob = expo / jnp.sum(expo, axis=0, keepdims=True)
            probs[k, t] = prob
            grad = dot(unfold(prob, block), heads(u[k], t), (1, 0))
            grad_v[t * TILE : (t + 1) * TILE, k * HD : (k + 1) * HD] = grad.astype(BF16)


def dscore_kernel(probs, values, upstream, queries, keys, grad_q, grad_k, token):
    finish(token)
    scale = 1.0 / HD**0.5
    block = own_block(GROUP * TILE)
    for t in range(probs.shape[1]):
        rows = slice(t * TILE, (t + 1) * TILE)
        prob = probs[0, t]
        dprob = fold(dot(values[rows, :], heads(upstream, t), (1, 1)), block)
        delta = jnp.sum(prob * dprob, axis=0, keepdims=True)
        dscore = unfold(prob * (dprob - delta), block)
        grad_k[rows, :] = (dot(dscore, heads(queries, t), (1, 0)) * scale).astype(BF16)
        grad = (dot(dscore, keys[rows, :], (0, 0)) * scale).astype(BF16)
        for h in range(GROUP):
            grad_q[rows, h * HD : (h + 1) * HD] = grad[h * TILE : (h + 1) * TILE]


def per_head(kernel, name, ins, outs, args, flops):
    size = sum(a.size * a.dtype.itemsize for a in args) + sum(o.size * o.dtype.itemsize for o, _ in outs)
    return pl.pallas_call(
        kernel,
        grid=(KVH,),
        out_shape=[o for o, _ in outs],
        in_specs=ins,
        out_specs=[s for _, s in outs],
        compiler_params=pltpu.CompilerParams(vmem_limit_bytes=56 * 1024 * 1024),
        cost_estimate=pl.CostEstimate(flops=flops, bytes_accessed=size, transcendentals=0),
        name=name,
    )(*args)


def attention_specs(slots):
    wide = pl.BlockSpec((slots, GROUP * HD), lambda k: (0, k))
    narrow = pl.BlockSpec((slots, HD), lambda k: (0, k))
    tiles = slots // TILE
    folded = pl.BlockSpec((1, tiles, CAP, GROUP * TILE), lambda k: (k, 0, 0, 0))
    return wide, narrow, folded, like((KVH, tiles, CAP, GROUP * TILE), F32)


def folded_shape(slots):
    return (KVH, slots // TILE, CAP, GROUP * TILE)


def attention_scores(queries, keys):
    slots = queries.shape[0]
    sems = pltpu.SemaphoreType.DMA((1 + KVH,))
    scratch = (pltpu.VMEM((KVH, slots, GROUP * HD), BF16), pltpu.VMEM(keys.shape, BF16), sems)
    out = [like(folded_shape(slots), F32)]
    flops = 2 * queries.size * TILE
    return call(scores_kernel, "scores", out, queries, keys, ins=[ANY] * 2, scratch=scratch, mib=56, flops=flops)[0]


def attention_probs(scores, masks, upstream, after):
    slots = upstream.shape[0]
    u = pltpu.VMEM((KVH, slots, GROUP * HD), BF16)
    sems = pltpu.SemaphoreType.DMA((2 + KVH,))
    scratch = (u, pltpu.VMEM(scores.shape, F32), pltpu.VMEM(masks.shape, jnp.int32), sems)
    out = [like((slots, KVH * HD), BF16), like(scores.shape, F32)]
    flops = 2 * upstream.size * TILE
    ins = [ANY] * (3 + len(after))
    return call(probs_kernel, "probs", out, scores, masks, upstream, *after, ins=ins, scratch=scratch, mib=56, flops=flops)


def attention_dscore(probs, values, upstream, queries, keys):
    wide, narrow, folded, _ = attention_specs(queries.shape[0])
    token = (TOKEN, pl.BlockSpec(TOKEN.shape, lambda k: (0, 0)))
    outs = [(like(queries.shape, BF16), wide), (like(keys.shape, BF16), narrow), token]
    args = (probs, values, upstream, queries, keys)
    flops = 6 * upstream.size * TILE
    return per_head(dscore_kernel, "dscore", [folded, narrow, wide, wide, narrow], outs, args, flops)


def slice_of(weights, s):
    half = weights.shape[1] // NZH
    rows = slice(s // NX * half, (s // NX + 1) * half)
    return jnp.concatenate([weights[cr * NX + s % NX, rows] for cr in range(NCO)], axis=0)


def partial_kernel(*refs):
    ins, (_, v0, v1, v2, v3, x, w, sems) = refs[: NY + SLICES], refs[NY + SLICES :]
    rows, width = x.shape[1], w.shape[1]
    copies = fetch(ins, [x.at[k] for k in range(NY)] + [w.at[i] for i in range(SLICES)], sems)
    for copy in copies:
        copy.wait()
    total = None
    for s in range(SLICES):
        stack = jnp.concatenate([x[k, :, s * width : (s + 1) * width] for k in range(NY)], axis=0)
        term = dot(stack, slice_of(w, s), (1, 0))
        total = term if total is None else total + term
    for k, out in enumerate((v0, v1, v2, v3)):
        out[...] = total[k * rows : (k + 1) * rows].astype(out.dtype)


def staged(*groups):
    stacks = [pltpu.VMEM((len(g), *g[0].shape), g[0].dtype) for g in groups]
    return (*stacks, pltpu.SemaphoreType.DMA((sum(map(len, groups)),)))


def partial_values(pieces, weights, after):
    rows, width = pieces[0].shape[0], weights[0].shape[1]
    out = [like((rows, width), F32)] + [like((rows, width), BF16)] * (NY - 1)
    flops = 2 * NY * pieces[0].size * width
    ins, scratch = [ANY] * (NY + SLICES + 1), staged(pieces, weights)
    return call(partial_kernel, "partial_values", out, *pieces, *weights, after, ins=ins, scratch=scratch, mib=56, flops=flops)


def place_kernel(slot, own, a, b, c, after, out):
    rows = own[...] + a[...].astype(F32) + b[...].astype(F32) + c[...].astype(F32)
    at = lax.broadcasted_iota(jnp.int32, (out.shape[0], own.shape[0]), 0)
    chosen = jnp.where(at == slot[...], 1.0, 0.0).astype(BF16)
    out[...] = dot(chosen, rows.astype(BF16), (1, 0)).astype(BF16)


def pick_kernel(*refs):
    slot, buffer, out = refs[0], refs[1], refs[-1]
    at = lax.broadcasted_iota(jnp.int32, (buffer.shape[0], out.shape[0]), 0)
    chosen = jnp.where(at == slot[...], 1.0, 0.0).astype(BF16)
    out[...] = dot(chosen, buffer[...], (0, 0)).astype(BF16)


def back_kernel(*refs):
    ins, (_, g0, g1, g2, g3, token, r, w, sems) = refs[: NY + SLICES], refs[NY + SLICES :]
    finish(token)
    rows, width = r.shape[1], w.shape[1]
    copies = fetch(ins, [r.at[k] for k in range(NY)] + [w.at[i] for i in range(SLICES)], sems)
    for copy in copies:
        copy.wait()
    stack = r[...].reshape(NY * rows, r.shape[2])
    for s in range(SLICES):
        grad = dot(stack, slice_of(w, s), (1, 1)).astype(BF16)
        for k, out in enumerate((g0, g1, g2, g3)):
            out[:, s * width : (s + 1) * width] = grad[k * rows : (k + 1) * rows]


def back(grads, weights, after):
    rows, width = grads[0].shape
    columns = SLICES * weights[0].shape[0]
    flops = 2 * NY * rows * width * columns
    ins, scratch = [ANY] * (NY + SLICES + 1), staged(grads, weights)
    out = [like((rows, columns), BF16)] * NY + [TOKEN]
    return call(back_kernel, "back", out, *grads, *weights, after, ins=ins, scratch=scratch, mib=56, flops=flops)


def share_kernel(*refs):
    ins, (own, other, token, x, r, sems) = refs[: 2 * NY], refs[-6:]
    finish(token)
    half = own.shape[1]
    copies = fetch(ins, [x.at[k] for k in range(NY)] + [r.at[k] for k in range(NY)], sems)
    for copy in copies:
        copy.wait()
    grads = r[...].reshape(NY * r.shape[1], r.shape[2])
    for s in range(SLICES):
        stack = jnp.concatenate([x[k, :, s * NCO * half : (s + 1) * NCO * half] for k in range(NY)], axis=0)
        share = dot(stack, grads, (0, 0))
        own[s] = share[:half]
        other[s] = share[half:].astype(other.dtype)


def shares(pieces, grads, after):
    half, width = pieces[0].shape[1] // SLICES // NCO, grads[0].shape[1]
    shape = (SLICES, half, width)
    flops = 2 * NY * pieces[0].size * width
    out = [like(shape, F32), like(shape, BF16), TOKEN]
    ins, scratch = [ANY] * (2 * NY + len(after)), staged(pieces, grads)
    return call(share_kernel, "shares", out, *pieces, *grads, *after, ins=ins, scratch=scratch, mib=20, flops=flops)


def core_sum_kernel(own, got, keep, s1, s2, s3):
    for zr in range(NZH):
        for xr, out in enumerate((keep, s1, s2, s3)):
            out[zr] = (own[zr * NX + xr] + got[zr * NX + xr].astype(F32)).astype(out.dtype)


def x_sum_kernel(keep, a, b, c, after, near, far):
    for zr, out in enumerate((near, far)):
        total = keep[zr] + a[zr].astype(F32) + b[zr].astype(F32) + c[zr].astype(F32)
        out[...] = total.astype(out.dtype)


def stack_kernel(a, b, out):
    rows = a.shape[0] // NCO
    here = pl.ds(pl.multiple_of(at_place()[0] * rows, rows), rows)
    out[:rows] = a[here, :]
    out[rows:] = b[here, :]


def pair_sum_kernel(*refs):
    a, b, out = refs[0], refs[1], refs[-1]
    out[...] = (a[...].astype(F32) + b[...].astype(F32)).astype(out.dtype)


def halves_kernel(mine, other, after, out):
    core, rows = at_place()[0], mine.shape[0]
    out[pl.ds(pl.multiple_of(core * rows, rows), rows), :] = mine[...]
    out[pl.ds(pl.multiple_of((1 - core) * rows, rows), rows), :] = other[...]


def body(inputs, value_weight, send_slot, response_id, queries, keys, upstream):
    peers = lax.axis_size("fsdp")
    slots, rows = queries.shape[0], inputs.shape[0]
    half, width = value_weight.shape[0] // NCO, value_weight.shape[1]
    slot = send_slot.reshape(1, rows)

    def exchange(buffer):
        return lax.all_to_all(buffer, "fsdp", split_axis=0, concat_axis=0, tiled=True)

    mask = run_masks(send_slot, response_id, peers)
    masks = exchange(mask)
    mirrored = permute(value_weight, mirror)
    pieces = split(inputs, mask)
    pieces = [pieces[0]] + [permute(pieces[k], along_y(k)) for k in range(1, NY)]
    pair = call(stack_kernel, "pair", [like((NZH * half, width), BF16)], value_weight, mirrored)[0]
    weights = [pair] + [permute(pair, along_x(k)) for k in range(1, NX)]
    weights += [permute(weight, other_core) for weight in weights]

    scores = attention_scores(queries, keys)
    grad_v, probs = attention_probs(scores, masks, upstream, (pair,))
    returned = exchange(grad_v)
    order, out = [VMEM] * 2 + [ANY] * (NY - 1), [like((rows, width), BF16)]
    row_grad = call(pick_kernel, "pick", out, slot, returned, *pieces[1:], ins=order)[0]
    grads = [row_grad] + [permute(row_grad, along_y(k)) for k in range(1, NY)]

    own, other, shared = shares(pieces, grads, weights[1:NX])
    partial, *parts = partial_values(pieces, weights, shared)
    parts = [permute(part, along_y(-k)) for k, part in enumerate(parts, 1)]
    got = permute(other, other_core)
    out = [like((NZH, half, width), F32)] + [like((NZH, half, width), BF16)] * (NX - 1)
    keep, *sends = call(core_sum_kernel, "core_sum", out, own, got, mib=8)
    arrived = [permute(send, along_x(-k)) for k, send in enumerate(sends, 1)]

    mine, *sends, backed = back(grads, weights, keep)
    columns = [mine] + [permute(send, along_y(-k)) for k, send in enumerate(sends, 1)]

    out = [like((half, width), F32), like((half, width), BF16)]
    near, far = call(x_sum_kernel, "x_sum", out, keep, *arrived, backed, ins=[VMEM] * NX + [ANY])
    small, order = [like((half, width), BF16)], [VMEM, VMEM, ANY]
    total = call(pair_sum_kernel, "mirror_sum", small, near, permute(far, mirror), *parts, ins=[VMEM] * 2 + [ANY] * (NY - 1))[0]

    after, out = [VMEM] * 5 + [ANY], [like((slots, width), BF16)]
    value_buffer = call(place_kernel, "place", out, slot, partial, *parts, total, ins=after)[0]
    values = exchange(value_buffer)
    grad_q, grad_k, scored = attention_dscore(probs, values, upstream, queries, keys)
    grad_inputs, joined = join(columns)

    after = [VMEM] * 2 + [ANY] * 2
    total = call(pair_sum_kernel, "z_sum", small, total, permute(total, flip_zl(1)), columns[1], columns[3], ins=after)[0]
    total = call(pair_sum_kernel, "z_sum", small, total, permute(total, flip_zl(2)), scored, ins=order)[0]
    out = [like((NCO * half, width), BF16)]
    grad_weight = call(halves_kernel, "halves", out, total, permute(total, other_core), joined, ins=order)[0]
    return grad_inputs, grad_q, grad_k, grad_weight


def solution(mesh):
    spread, sharded = P(("rep", "fsdp"), None), P("fsdp", None)
    line = P(("rep", "fsdp"))
    return jax.shard_map(
        body,
        mesh=mesh,
        in_specs=(spread, sharded, line, line, spread, spread, spread),
        out_specs=(spread, spread, spread, sharded),
        check_vma=False,
    )
```
